256 devices in a mesh: pass: 64 (over y, z, core), tensor: 4 (over x).
Axes of the slice: x: 4, y: 4, z: 8, core: 2. Of those that a mesh axis runs over, the one named last changes fastest.
Arguments:
- queries: bfloat16 [8192, 4096], P('pass', 'tensor'), may hold values from -3 to 3
- keys_values: bfloat16 [128, 32, 2, 4096], P('pass', None, None, 'tensor'), may hold values from -4 to 4
- out_weight: bfloat16 [4096, 4096], P('tensor'), may hold values from -0.375 to 0.375
- cotangent: bfloat16 [8192, 4096], P('pass', 'tensor'), may hold values from -6 to 6
- retrieval: int32 [64, 32], replicated, may hold values from 0 to 127, as said below
- lengths: int32 [64], P('pass'), may hold values from 1 to 128
Outputs:
- attended: bfloat16 [8192, 4096], P('pass', 'tensor')
- grad_queries: bfloat16 [8192, 4096], P('pass', 'tensor')
- grad_keys_values: bfloat16 [128, 32, 2, 4096], P('pass', None, None, 'tensor')
The draws below stay inside these ranges and needn't reach their ends.
Inputs may be any that keep to these rules, and one draw needn't show every extreme that they name: `retrieval`: row q lists 32 different passage ids; passage p is held by the device of index p // 2 along pass, and no row lists two passages of the same device.
All inputs are finite; a program needn't handle non-finite values.
Results may differ from the reference program's by a relative error of at most 0.015.
Values may be sent and summed in bfloat16 or wider, within the bound.
A program may use at most 128 MiB of HBM per device.

```python
import jax
import jax.numpy as jnp
from jax import lax

D = 4096
HEADS = 64
HS = 64
TGT = 128
LEN = 32
PDEV = 2
HD = 4096
QUESTIONS = 64
PASSAGES = 128
K_RET = 32


def draw_queries(key, part):
    key = jax.random.fold_in(key, 21)
    base = jnp.clip(0.25 * jax.random.normal(key, (QUESTIONS * TGT, HD), jnp.float32), -1.5, 1.5)
    return base.astype(jnp.bfloat16)


def draw_keys_values(key, part):
    key = jax.random.fold_in(key, 33)
    base = jnp.clip(jax.random.normal(key, (PASSAGES, LEN, 2, HD), jnp.float32), -4.0, 4.0)
    return base.astype(jnp.bfloat16)


def draw_retrieval(key, part):
    key = jax.random.fold_in(key, 45)
    shard_count = PASSAGES // PDEV
    perm_keys = jax.random.split(jax.random.fold_in(key, 1), QUESTIONS)
    shard_lists = jax.vmap(lambda one: jax.random.permutation(one, shard_count)[:K_RET])(perm_keys)
    first = jax.random.randint(jax.random.fold_in(key, 2), (QUESTIONS, K_RET), 0, PDEV)
    second = jax.random.randint(jax.random.fold_in(key, 3), (QUESTIONS, K_RET), 0, PDEV)
    local_pick = jnp.minimum(first, second)
    forced = jax.random.randint(jax.random.fold_in(key, 4), (), 0, QUESTIONS)
    other = (forced + 1) % QUESTIONS
    slot_ids = jnp.arange(K_RET)
    top_shards = shard_count - 1 - slot_ids
    question_ids = jnp.arange(QUESTIONS)[:, None]
    shard_lists = jnp.where(question_ids == forced, top_shards[None, :], shard_lists)
    shard_lists = jnp.where(question_ids == other, slot_ids[None, :], shard_lists)
    local_pick = jnp.where((question_ids == forced) & (slot_ids[None, :] == 0), PDEV - 1, local_pick)
    local_pick = jnp.where((question_ids == other) & (slot_ids[None, :] == 0), 0, local_pick)
    return (shard_lists * PDEV + local_pick).astype(jnp.int32)


def draw_lengths(key, part):
    key = jax.random.fold_in(key, 57)
    drawn = jax.random.randint(jax.random.fold_in(key, 1), (QUESTIONS,), 1, TGT + 1)
    forced = jax.random.randint(jax.random.fold_in(key, 2), (), 0, QUESTIONS)
    return jnp.where(jnp.arange(QUESTIONS) == forced, TGT, drawn).astype(jnp.int32)


def block_scale(own_key, shape, shards, least, top_value):
    factor_of, own = 1.0, jax.random.fold_in(own_key, 6)
    for axis_at, shards_of in shards:
        heights = jnp.exp(jax.random.uniform(jax.random.fold_in(own, axis_at), (shards_of,), jnp.float32, least / len(shards), top_value / len(shards)))
        factor_of = factor_of * jnp.repeat(heights, shape[axis_at] // shards_of).reshape([-1 if axis == axis_at else 1 for axis in range(len(shape))])
    return factor_of


def gaussian(rng, shape, scale, most, cuts=(), kind=jnp.bfloat16):
    loudness = block_scale(rng, shape, cuts, -0.22, 0.18) if cuts else 1.0
    values = jax.random.normal(rng, shape, jnp.float32) * scale * loudness
    return jnp.minimum(jnp.maximum(values, -most), most).astype(kind)


def setup_inputs(seed: int = 0) -> dict:
    streams_of = jax.random.split(jax.random.key(seed), 7)
    return {
        "queries": draw_queries(jax.random.fold_in(streams_of[6], 71), 0),
        "keys_values": draw_keys_values(jax.random.fold_in(streams_of[6], 71), 0),
        "out_weight": gaussian(streams_of[2], (HD, D), (HD // 16) ** -0.5, 0.375, ((0, 4),)),
        "cotangent": gaussian(streams_of[3], (QUESTIONS * TGT, D), 1.0, 6.0, ((0, 64), (1, 4))),
        "retrieval": draw_retrieval(jax.random.fold_in(streams_of[6], 71), 0),
        "lengths": draw_lengths(jax.random.fold_in(streams_of[6], 71), 0),
    }


def softmax_rows(scores):
    row_max = jnp.max(scores, axis=-1, keepdims=True)
    raised = jnp.exp(scores - row_max)
    return raised / jnp.sum(raised, axis=-1, keepdims=True)


def question_terms(query_rows, passage_rows, out_weight, cot_rows, live_rows):
    key_count = passage_rows.shape[0]
    query_full = query_rows.astype(jnp.float32).reshape(TGT, HEADS, HS)
    key_full = passage_rows[:, 0, :].astype(jnp.float32).reshape(key_count, HEADS, HS)
    value_full = passage_rows[:, 1, :].astype(jnp.float32).reshape(key_count, HEADS, HS)
    scores = jnp.einsum("thd,rhd->htr", query_full, key_full)
    prob_full = softmax_rows(scores)
    prob_half = lax.optimization_barrier(prob_full.astype(jnp.bfloat16)).astype(jnp.float32)
    context = jnp.einsum("htr,rhd->thd", prob_half, value_full).reshape(TGT, HD).astype(jnp.bfloat16)
    mixed = jnp.dot(context, out_weight, preferred_element_type=jnp.float32)
    attended = jnp.where(live_rows[:, None], mixed, 0.0).astype(jnp.bfloat16)
    masked_cot = jnp.where(live_rows[:, None], cot_rows, jnp.zeros_like(cot_rows))
    grad_context = jnp.dot(masked_cot, out_weight.T, preferred_element_type=jnp.float32).astype(jnp.bfloat16)
    grad_full = lax.optimization_barrier(grad_context).astype(jnp.float32).reshape(TGT, HEADS, HS)
    grad_prob = jnp.einsum("thd,rhd->htr", grad_full, value_full)
    grad_scores = prob_full * (grad_prob - jnp.sum(grad_prob * prob_full, axis=-1, keepdims=True))
    grad_scores = lax.optimization_barrier(grad_scores.astype(jnp.bfloat16)).astype(jnp.float32)
    grad_query = jnp.einsum("htr,rhd->thd", grad_scores, key_full).reshape(TGT, HD).astype(jnp.bfloat16)
    grad_key = jnp.einsum("htr,thd->rhd", grad_scores, query_full).reshape(key_count, HD).astype(jnp.bfloat16)
    grad_value = jnp.einsum("htr,thd->rhd", prob_half, grad_full).reshape(key_count, HD).astype(jnp.bfloat16)
    return attended, grad_query, jnp.stack([grad_key, grad_value], axis=1)


def reference(queries, keys_values, out_weight, cotangent, retrieval, lengths):
    positions = jnp.arange(TGT, dtype=jnp.int32)

    def per_question(running, question):
        passage_ids = retrieval[question]
        passage_rows = keys_values[passage_ids].reshape(K_RET * LEN, 2, HD)
        query_rows = lax.dynamic_slice_in_dim(queries, question * TGT, TGT, 0)
        cot_rows = lax.dynamic_slice_in_dim(cotangent, question * TGT, TGT, 0)
        live_rows = positions < lengths[question]
        attended, grad_query, slot_grads = question_terms(query_rows, passage_rows, out_weight, cot_rows, live_rows)
        running = running.at[passage_ids].add(slot_grads.reshape(K_RET, LEN, 2, HD).astype(jnp.float32))
        return running, (attended, grad_query)

    start = jnp.zeros((PASSAGES, LEN, 2, HD), jnp.float32)
    summed, (attended, grad_query) = lax.scan(per_question, start, jnp.arange(QUESTIONS, dtype=jnp.int32))
    return (attended.reshape(QUESTIONS * TGT, D), grad_query.reshape(QUESTIONS * TGT, HD), summed.astype(jnp.bfloat16))
```

```python
import functools

import jax
import jax.numpy as jnp
from jax import lax
from jax.experimental import pallas as pl
from jax.experimental.pallas import tpu as pltpu
from jax.sharding import PartitionSpec as P

HS = 64
PAIR = 2 * HS
CORES = 2
CHUNKS = 4
MESH = pl.DeviceIdType.MESH
NT = (((1,), (1,)), ((), ()))
TN = (((0,), (0,)), ((), ()))
NN = (((1,), (0,)), ((), ()))


def dot(a, b, dims):
    return lax.dot_general(a, b, dims, preferred_element_type=jnp.float32)


def kernel(
    nx,
    ny,
    nz,
    ids_ref,
    inv_ref,
    len_ref,
    q_ref,
    kv_ref,
    w_ref,
    cot_ref,
    att_ref,
    gq_ref,
    gkv_ref,
    kvbuf,
    qbuf,
    gbuf,
    cotbuf,
    wbuf,
    gacc,
    gsend,
    kvg,
    ebuf,
    dsbuf,
    stbuf,
    ctxt,
    invl,
    csend,
    ctxbuf,
    qsend,
    sg,
    asend,
    arecv,
    aown,
    cxs,
    cxr,
    ysend,
    yrecv,
    ysum,
    zsend,
    loc_sem,
    kz_s,
    kz_r,
    ky_s,
    ky_r,
    kc_s,
    kc_r,
    q_s,
    q_r,
    g_s,
    g_r,
    c_s,
    c_r,
    d_s,
    d_r,
    x_s,
    x_r,
    a_s,
    a_r,
    e_s,
    e_r,
    f_s,
    f_r,
    o_s,
    o_r,
):
    nc = CORES
    rows = q_ref.shape[0]
    cols = q_ref.shape[1]
    pdev, plen, width = kv_ref.shape[1:]
    slots = ids_ref.shape[1]
    keys = slots * plen
    chunks = min(CHUNKS, nz)
    zper = nz // chunks
    me = lax.axis_index("pass")
    x = lax.axis_index("tensor")
    c = lax.rem(me, nc)
    z = lax.rem(me // nc, nz)
    y = me // (nc * nz)
    oc = 1 - c

    def at(yy, zz, cc):
        return (yy * nz + zz) * nc + cc

    def turn(t):
        half = (t + 1) // 2
        return jnp.where(lax.rem(t, 2) == 1, half, -half)

    def zat(t):
        return lax.rem(z + turn(t) + nz, nz)

    def yat(t):
        return lax.rem(y + turn(t) + ny, ny)

    def xat(t):
        return lax.rem(x + turn(t) + nx, nx)

    def place(yy, cc, zz):
        return ((yy * nc + cc) * nz + zz) * pdev

    def remote(src, dst, send, recv, dev):
        return pltpu.make_async_remote_copy(
            src_ref=src,
            dst_ref=dst,
            send_sem=send,
            recv_sem=recv,
            device_id=dev,
            device_id_type=MESH,
        )

    def each(lo, hi, body):
        lax.fori_loop(lo, hi, lambda t, carry: (body(t), carry)[1], 0)

    def lanes(i):
        return pl.ds(pl.multiple_of(i * PAIR, PAIR), PAIR)

    def kz_copy(zt, zs):
        return remote(
            kv_ref.at[zt],
            kvbuf.at[pl.ds(place(y, c, zs), pdev)],
            kz_s.at[zt],
            kz_r.at[zs],
            (at(y, zt, c), x),
        )

    def ky_copy(yt, ys, i):
        part = pl.ds(place(ys, c, i * zper), zper * pdev)
        return remote(
            kvbuf.at[part],
            kvbuf.at[part],
            ky_s.at[yt * chunks + i],
            ky_r.at[ys * chunks + i],
            (at(yt, z, c), x),
        )

    def kc_copy(ys, cs, i):
        part = pl.ds(place(ys, cs, i * zper), zper * pdev)
        return remote(
            kvbuf.at[part],
            kvbuf.at[part],
            kc_s.at[ys * chunks + i],
            kc_r.at[ys * chunks + i],
            (at(y, z, oc), x),
        )

    def q_copy(zt, zs):
        return remote(
            q_ref.at[:, lanes(zt)], qbuf.at[zs], q_s.at[zt], q_r.at[zs], (at(y, zt, c), x)
        )

    def g_copy(zt, zs):
        return remote(
            gsend.at[zt], gbuf.at[zs], g_s.at[zt], g_r.at[zs], (at(y, zt, c), x)
        )

    def c_copy(zt, zs):
        return remote(
            csend.at[zt], ctxbuf.at[:, lanes(zs)], c_s.at[zt], c_r.at[zs], (at(y, zt, c), x)
        )

    def d_copy(zt, zs):
        return remote(
            qsend.at[zt], gq_ref.at[:, lanes(zs)], d_s.at[zt], d_r.at[zs], (at(y, zt, c), x)
        )

    def x_copy(xt, xs):
        return remote(cot_ref, cotbuf.at[xs], x_s.at[xt], x_r.at[xs], (me, xt))

    def a_copy(xt, xs):
        return remote(asend.at[xt], arecv.at[xs], a_s.at[xt], a_r.at[xs], (me, xt))

    def e_copy(yt):
        return remote(cxs.at[yt], cxr.at[yt], e_s.at[yt], e_r.at[yt], (at(y, z, oc), x))

    def f_copy(yt, ys):
        return remote(ysend.at[yt], yrecv.at[ys], f_s.at[yt], f_r.at[ys], (at(yt, z, c), x))

    def o_copy(zt, zs):
        return remote(zsend.at[zt], gkv_ref.at[zs], o_s.at[zt], o_r.at[zs], (at(y, zt, c), x))

    w_load = pltpu.make_async_copy(w_ref, wbuf, loc_sem.at[0])
    kv_own = pltpu.make_async_copy(
        kv_ref.at[z], kvbuf.at[pl.ds(place(y, c, z), pdev)], loc_sem.at[1]
    )
    q_own = pltpu.make_async_copy(q_ref.at[:, lanes(z)], qbuf.at[z], loc_sem.at[2])
    cot_own = pltpu.make_async_copy(cot_ref, cotbuf.at[x], loc_sem.at[3])
    gq_own = pltpu.make_async_copy(qsend.at[z], gq_ref.at[:, lanes(z)], loc_sem.at[4])
    gkv_own = pltpu.make_async_copy(zsend.at[z], gkv_ref.at[z], loc_sem.at[5])

    barrier = pltpu.get_barrier_semaphore()

    def greet(dev):
        pl.semaphore_signal(barrier, inc=1, device_id=dev, device_id_type=MESH)

    each(1, nz, lambda t: greet((at(y, zat(t), c), x)))
    each(1, ny, lambda t: greet((at(yat(t), z, c), x)))
    each(1, nx, lambda t: greet((me, xat(t))))
    greet((at(y, z, oc), x))
    kv_own.start()
    cot_own.start()
    q_own.start()
    w_load.start()
    pl.semaphore_wait(barrier, nz + ny + nx - 2)

    each(1, nx, lambda t: x_copy(xat(t), x).start())
    each(1, nz, lambda t: kz_copy(zat(t), z).start())
    each(1, nz, lambda t: q_copy(zat(t), z).start())

    live = lax.broadcasted_iota(jnp.int32, (rows, 1), 0) < len_ref[0]
    low_lane = lax.broadcasted_iota(jnp.int32, (1, PAIR), 1) < HS
    low_row = lax.broadcasted_iota(jnp.int32, (PAIR, 1), 0) < HS
    blank = jnp.zeros((1, 1), jnp.bfloat16)

    sg_zero = jnp.zeros((plen, width), jnp.bfloat16)

    def clear(j):
        sg[j, slots] = sg_zero

    each(0, nz, clear)

    step = 256
    cot_own.wait()
    w_load.wait()

    def grad_part(xs, first):
        block = cotbuf[xs]

        def one(n):
            at_n = pl.ds(pl.multiple_of(n * step, step), step)
            weight = wbuf[at_n, pl.ds(pl.multiple_of(xs * cols, cols), cols)]
            part = dot(block, weight, NT)
            if first:
                gacc[:, at_n] = part
            else:
                gacc[:, at_n] += part

        each(0, cols // step, one)

    grad_part(x, True)

    kv_own.wait()

    def forward(i):
        def arrived(k):
            zs = i * zper + k

            @pl.when(zs != z)
            def _():
                kz_copy(zs, zs).wait_recv()

        each(0, zper, arrived)
        each(1, ny, lambda t: ky_copy(yat(t), y, i).start())
        kc_copy(y, c, i).start()

    each(0, chunks, forward)

    def other_part(t):
        xs = xat(t)
        x_copy(xs, xs).wait_recv()
        grad_part(xs, False)

    each(1, nx, other_part)
    for h in range(nz):
        gsend[h] = jnp.where(live, gacc[:, h * PAIR : (h + 1) * PAIR], 0.0).astype(jnp.bfloat16)
    gbuf[z] = gsend[z]
    each(1, nz, lambda t: g_copy(zat(t), z).start())

    def pass_on(t):
        ys = yat(t)

        def one(i):
            ky_copy(ys, ys, i).wait_recv()
            kc_copy(ys, c, i).start()

        each(0, chunks, one)

    each(1, ny, pass_on)
    each(0, ny * chunks, lambda k: kc_copy(k // chunks, oc, lax.rem(k, chunks)).wait_recv())

    q_own.wait()
    tile = 256
    tiles = keys // tile

    def both_rows(block):
        return jnp.concatenate(
            [jnp.where(low_lane, block, blank), jnp.where(low_lane, blank, block)], axis=0
        )

    def both_cols(block):
        return jnp.concatenate(
            [jnp.where(low_row, block, blank), jnp.where(low_row, blank, block)], axis=1
        )

    def pick(wide):
        return jnp.where(low_row, wide[:, :rows], wide[:, rows:])

    def attend(t):
        j = zat(t)

        @pl.when(t > 0)
        def _():
            q_copy(j, j).wait_recv()

        for k in range(slots):
            kvg[j, k * plen : (k + 1) * plen, :] = kvbuf[ids_ref[j, k]]
        query = both_rows(qbuf[j])
        top = jnp.full((1, 2 * rows), -jnp.inf, jnp.float32)
        for r in range(tiles):
            at_r = pl.ds(r * tile, tile)
            part = dot(kvg[j, at_r, :PAIR], query, NT)
            stbuf[at_r, :] = part
            top = jnp.maximum(top, jnp.max(part, axis=0, keepdims=True))
        total = jnp.zeros((1, 2 * rows), jnp.float32)
        for r in range(tiles):
            at_r = pl.ds(r * tile, tile)
            raised = jnp.exp(stbuf[at_r, :] - top)
            total = total + jnp.sum(raised, axis=0, keepdims=True)
            ebuf[j, at_r, :] = raised.astype(jnp.bfloat16)
        inverse = 1.0 / total
        mixed = dot(kvg[j, :, PAIR:], ebuf[j], TN) * inverse
        mixed = pick(mixed)
        ctxt[j] = mixed
        invl[j] = inverse
        csend[j] = mixed.T.astype(jnp.bfloat16)

        @pl.when(t > 0)
        def _():
            c_copy(j, z).start()

    each(0, nz, attend)
    ctxbuf[:, lanes(z)] = csend[z]

    def grads(t):
        j = zat(t)

        @pl.when(t > 0)
        def _():
            g_copy(j, j).wait_recv()

        query = both_rows(qbuf[j])
        inverse = jnp.where(low_row, invl[j, :, :rows], invl[j, :, rows:])
        scaled = gbuf[j].astype(jnp.float32).T * inverse
        product = scaled * ctxt[j]
        delta = jnp.concatenate(
            [
                jnp.sum(product[:HS], axis=0, keepdims=True),
                jnp.sum(product[HS:], axis=0, keepdims=True),
            ],
            axis=1,
        )
        wide = both_cols(scaled.astype(jnp.bfloat16))
        for r in range(tiles):
            at_r = pl.ds(r * tile, tile)
            raised = ebuf[j, at_r, :]
            grad = dot(kvg[j, at_r, PAIR:], wide, NN)
            grad = (raised.astype(jnp.float32) * (grad - delta)).astype(jnp.bfloat16)
            dsbuf[at_r, :] = grad
            per = tile // plen
            key_grad = dot(grad, query, NN).astype(jnp.bfloat16)
            value_grad = dot(raised, wide, NT).astype(jnp.bfloat16)
            sg[j, r * per : (r + 1) * per, :, :PAIR] = key_grad.reshape(per, plen, PAIR)
            sg[j, r * per : (r + 1) * per, :, PAIR:] = value_grad.reshape(per, plen, PAIR)
        back = pick(dot(kvg[j, :, :PAIR], dsbuf[...], TN))
        qsend[j] = back.T.astype(jnp.bfloat16)

        @pl.when(t > 0)
        def _():
            d_copy(j, z).start()

    each(0, nz // 2, grads)

    each(1, nz, lambda t: c_copy(zat(t), zat(t)).wait_recv())

    def project(xt, own):
        def one(n):
            at_n = pl.ds(pl.multiple_of(n * step, step), step)
            weight = wbuf[:, pl.ds(pl.multiple_of(xt * cols + n * step, step), step)]
            part = jnp.where(live, dot(ctxbuf[...], weight, NN), 0.0)
            if own:
                aown[:, at_n] = part
            else:
                asend[xt, :, at_n] = part.astype(jnp.bfloat16)

        each(0, cols // step, one)

    def project_other(t):
        xt = xat(t)
        project(xt, False)
        a_copy(xt, x).start()

    each(1, nx, project_other)
    project(x, True)
    each(nz // 2, nz, grads)
    gq_own.start()

    def gather(p):
        total = sg[0, inv_ref[0, p]].astype(jnp.float32)
        for j in range(1, nz):
            total = total + sg[j, inv_ref[j, p]].astype(jnp.float32)
        return total

    per_y = nz * pdev

    def for_other_core(t):
        yt = yat(ny - 1 - t)

        def one(k):
            cxs[yt, k] = gather(place(yt, oc, 0) + k).astype(jnp.bfloat16)

        each(0, per_y, one)
        e_copy(yt).start()

    each(0, ny, for_other_core)

    def for_other_y(t):
        yt = yat(t)
        e_copy(yt).wait_recv()

        def one(k):
            total = gather(place(yt, c, 0) + k) + cxr[yt, k].astype(jnp.float32)
            ysend[yt, k] = total.astype(jnp.bfloat16)

        each(0, per_y, one)
        f_copy(yt, y).start()

    each(1, ny, for_other_y)
    e_copy(y).wait_recv()

    def own_y(k):
        ysum[k] = gather(place(y, c, 0) + k) + cxr[y, k].astype(jnp.float32)

    each(0, per_y, own_y)

    each(1, nx, lambda t: a_copy(xat(t), xat(t)).wait_recv())
    out = aown[...]
    for t in range(1, nx):
        out = out + arecv[xat(t)].astype(jnp.float32)
    att_ref[...] = out.astype(jnp.bfloat16)

    each(1, ny, lambda t: f_copy(yat(t), yat(t)).wait_recv())

    def finish(t):
        zt = zat(t)
        for k in range(pdev):
            total = ysum[zt * pdev + k]
            for s in range(1, ny):
                total = total + yrecv[yat(s), zt * pdev + k].astype(jnp.float32)
            zsend[zt, k] = total.astype(jnp.bfloat16)

        @pl.when(t > 0)
        def _():
            o_copy(zt, z).start()

    each(0, nz, lambda t: finish(nz - 1 - t))
    gkv_own.start()

    gq_own.wait()
    gkv_own.wait()

    def settle_z(t):
        zt = zat(t)
        d_copy(zt, zt).wait_recv()
        o_copy(zt, zt).wait_recv()
        kz_copy(zt, z).wait_send()
        q_copy(zt, z).wait_send()
        g_copy(zt, z).wait_send()
        c_copy(zt, z).wait_send()
        d_copy(zt, z).wait_send()
        o_copy(zt, z).wait_send()

    each(1, nz, settle_z)

    def settle_y(t):
        each(0, chunks, lambda i: ky_copy(yat(t), y, i).wait_send())
        f_copy(yat(t), y).wait_send()

    each(1, ny, settle_y)
    each(0, ny * chunks, lambda k: kc_copy(k // chunks, c, lax.rem(k, chunks)).wait_send())
    each(0, ny, lambda t: e_copy(t).wait_send())

    def settle_x(t):
        x_copy(xat(t), x).wait_send()
        a_copy(xat(t), x).wait_send()

    each(1, nx, settle_x)


def local(queries, keys_values, out_weight, cotangent, retrieval, lengths):
    pass_count = lax.axis_size("pass")
    nx = lax.axis_size("tensor")
    me = lax.axis_index("pass")
    pdev, plen, _, cols = keys_values.shape
    rows = queries.shape[0]
    width = out_weight.shape[1]
    slots = retrieval.shape[1]
    nz = cols // PAIR
    ny = pass_count // (nz * CORES)
    passages = pass_count * pdev
    keys = slots * plen

    own = lax.dynamic_slice(
        retrieval.reshape(ny, nz, CORES, slots),
        (me // (nz * CORES), 0, me % CORES, 0),
        (1, nz, 1, slots),
    ).reshape(nz, slots)
    holder = own // pdev
    hy, hz, hc = holder // (nz * CORES), (holder // CORES) % nz, holder % CORES
    ids = ((hy * CORES + hc) * nz + hz) * pdev + own % pdev
    match = ids[:, :, None] == jnp.arange(passages)[None, None, :]
    inverse = slots + jnp.sum(
        jnp.where(match, jnp.arange(slots)[None, :, None] - slots, 0), axis=1
    )
    pairs = (
        keys_values.reshape(pdev, plen, 2, nz, PAIR)
        .transpose(3, 0, 1, 2, 4)
        .reshape(nz, pdev, plen, 2 * PAIR)
    )

    bf, f32 = jnp.bfloat16, jnp.float32
    chunks = min(CHUNKS, nz)
    dma = pltpu.SemaphoreType.DMA
    vmem = pltpu.VMEM
    attended, grad_queries, grad_pairs = pl.pallas_call(
        functools.partial(kernel, nx, ny, nz),
        out_shape=(
            jax.ShapeDtypeStruct((rows, cols), bf),
            jax.ShapeDtypeStruct((rows, cols), bf),
            jax.ShapeDtypeStruct((nz, pdev, plen, 2 * PAIR), bf),
        ),
        in_specs=[pl.BlockSpec(memory_space=pltpu.SMEM)] * 3
        + [pl.BlockSpec(memory_space=pl.ANY)] * 4,
        out_specs=(
            pl.BlockSpec(memory_space=pltpu.VMEM),
            pl.BlockSpec(memory_space=pl.ANY),
            pl.BlockSpec(memory_space=pl.ANY),
        ),
        scratch_shapes=[
            vmem((passages, plen, 2 * PAIR), bf),
            vmem((nz, rows, PAIR), bf),
            vmem((nz, rows, PAIR), bf),
            vmem((nx, rows, cols), bf),
            vmem((cols, width), bf),
            vmem((rows, cols), f32),
            vmem((nz, rows, PAIR), bf),
            vmem((nz, keys, 2 * PAIR), bf),
            vmem((nz, keys, 2 * rows), bf),
            vmem((keys, 2 * rows), bf),
            vmem((keys, 2 * rows), f32),
            vmem((nz, PAIR, rows), f32),
            vmem((nz, 1, 2 * rows), f32),
            vmem((nz, rows, PAIR), bf),
            vmem((rows, cols), bf),
            vmem((nz, rows, PAIR), bf),
            vmem((nz, slots + 1, plen, 2 * PAIR), bf),
            vmem((nx, rows, cols), bf),
            vmem((nx, rows, cols), bf),
            vmem((rows, cols), f32),
            vmem((ny, nz * pdev, plen, 2 * PAIR), bf),
            vmem((ny, nz * pdev, plen, 2 * PAIR), bf),
            vmem((ny, nz * pdev, plen, 2 * PAIR), bf),
            vmem((ny, nz * pdev, plen, 2 * PAIR), bf),
            vmem((nz * pdev, plen, 2 * PAIR), f32),
            vmem((nz, pdev, plen, 2 * PAIR), bf),
            dma((6,)),
        ]
        + [dma((nz,))] * 2
        + [dma((ny * chunks,))] * 4
        + [dma((nz,))] * 8
        + [dma((nx,))] * 4
        + [dma((ny,))] * 4
        + [dma((nz,))] * 2,
        compiler_params=pltpu.CompilerParams(
            collective_id=0, has_side_effects=True, vmem_limit_bytes=48 * 1024 * 1024
        ),
    )(ids, inverse, lengths, queries, pairs, out_weight, cotangent)
    grad_keys_values = (
        grad_pairs.reshape(nz, pdev, plen, 2, PAIR)
        .transpose(1, 2, 3, 0, 4)
        .reshape(pdev, plen, 2, cols)
    )
    return (attended, grad_queries, grad_keys_values)


def solution(mesh):
    placed = (
        P("pass", "tensor"),
        P("pass", None, None, "tensor"),
        P("tensor", None),
        P("pass", "tensor"),
        P(),
        P("pass"),
    )
    return jax.shard_map(
        local,
        mesh=mesh,
        in_specs=placed,
        out_specs=(P("pass", "tensor"), P("pass", "tensor"), P("pass", None, None, "tensor")),
        check_vma=False,
    )
```

```python
import functools

import jax
import jax.numpy as jnp
from jax import lax
from jax.experimental import pallas as pl
from jax.experimental.pallas import tpu as pltpu
from jax.sharding import PartitionSpec as P

HS = 64
PAIR = 2 * HS
CORES = 2
CHUNKS = 4
MESH = pl.DeviceIdType.MESH
NT = (((1,), (1,)), ((), ()))
TN = (((0,), (0,)), ((), ()))
NN = (((1,), (0,)), ((), ()))


def dot(a, b, dims):
    return lax.dot_general(a, b, dims, preferred_element_type=jnp.float32)


def kernel(
    nx,
    ny,
    nz,
    ids_ref,
    inv_ref,
    len_ref,
    q_ref,
    kv_ref,
    w_ref,
    cot_ref,
    att_ref,
    gq_ref,
    gkv_ref,
    kvbuf,
    qbuf,
    gbuf,
    cotbuf,
    wbuf,
    gacc,
    gsend,
    kvg,
    ebuf,
    dsbuf,
    stbuf,
    ctxt,
    invl,
    csend,
    ctxbuf,
    qsend,
    sg,
    asend,
    arecv,
    aown,
    cxs,
    cxr,
    ysend,
    yrecv,
    zsend,
    loc_sem,
    kz_s,
    kz_r,
    ky_s,
    ky_r,
    kc_s,
    kc_r,
    q_s,
    q_r,
    g_s,
    g_r,
    c_s,
    c_r,
    d_s,
    d_r,
    x_s,
    x_r,
    a_s,
    a_r,
    e_s,
    e_r,
    f_s,
    f_r,
    o_s,
    o_r,
):
    nc = CORES
    rows = q_ref.shape[0]
    cols = q_ref.shape[1]
    pdev, plen, width = kv_ref.shape[1:]
    slots = ids_ref.shape[0]
    keys = slots * plen
    chunks = min(CHUNKS, nz)
    zper = nz // chunks
    me = lax.axis_index("pass")
    x = lax.axis_index("tensor")
    c = lax.rem(me, nc)
    z = lax.rem(me // nc, nz)
    y = me // (nc * nz)
    oc = 1 - c

    def at(yy, zz, cc):
        return (yy * nz + zz) * nc + cc

    def turn(t):
        half = (t + 1) // 2
        return jnp.where(lax.rem(t, 2) == 1, half, -half)

    def zat(t):
        return lax.rem(z + turn(t) + nz, nz)

    def yat(t):
        return lax.rem(y + turn(t) + ny, ny)

    def xat(t):
        return lax.rem(x + turn(t) + nx, nx)

    def place(yy, cc, zz):
        return ((yy * nc + cc) * nz + zz) * pdev

    def remote(src, dst, send, recv, dev):
        return pltpu.make_async_remote_copy(
            src_ref=src,
            dst_ref=dst,
            send_sem=send,
            recv_sem=recv,
            device_id=dev,
            device_id_type=MESH,
        )

    def each(lo, hi, body):
        lax.fori_loop(lo, hi, lambda t, carry: (body(t), carry)[1], 0)

    def lanes(i):
        return pl.ds(pl.multiple_of(i * PAIR, PAIR), PAIR)

    def kz_copy(zt, zs):
        return remote(
            kv_ref.at[zt],
            kvbuf.at[pl.ds(place(y, c, zs), pdev)],
            kz_s.at[zt],
            kz_r.at[zs],
            (at(y, zt, c), x),
        )

    def ky_copy(yt, ys, i):
        part = pl.ds(place(ys, c, i * zper), zper * pdev)
        return remote(
            kvbuf.at[part],
            kvbuf.at[part],
            ky_s.at[yt * chunks + i],
            ky_r.at[ys * chunks + i],
            (at(yt, z, c), x),
        )

    def kc_copy(ys, cs, i):
        part = pl.ds(place(ys, cs, i * zper), zper * pdev)
        return remote(
            kvbuf.at[part],
            kvbuf.at[part],
            kc_s.at[ys * chunks + i],
            kc_r.at[ys * chunks + i],
            (at(y, z, oc), x),
        )

    def q_copy(zt, zs):
        return remote(
            q_ref.at[:, lanes(zt)], qbuf.at[zs], q_s.at[zt], q_r.at[zs], (at(y, zt, c), x)
        )

    def g_copy(zt, zs):
        return remote(
            gsend.at[zt], gbuf.at[zs], g_s.at[zt], g_r.at[zs], (at(y, zt, c), x)
        )

    def c_copy(zt, zs):
        return remote(
            csend.at[zt], ctxbuf.at[:, lanes(zs)], c_s.at[zt], c_r.at[zs], (at(y, zt, c), x)
        )

    def d_copy(zt, zs):
        return remote(
            qsend.at[zt], gq_ref.at[:, lanes(zs)], d_s.at[zt], d_r.at[zs], (at(y, zt, c), x)
        )

    def x_copy(xt, xs):
        return remote(cot_ref, cotbuf.at[xs], x_s.at[xt], x_r.at[xs], (me, xt))

    def a_copy(xt, xs):
        return remote(asend.at[xt], arecv.at[xs], a_s.at[xt], a_r.at[xs], (me, xt))

    def e_copy(i):
        return remote(cxs.at[i], cxr.at[i], e_s.at[i], e_r.at[i], (at(y, z, oc), x))

    def f_copy(yt, ys, i):
        return remote(
            ysend.at[yt, i],
            yrecv.at[ys, i],
            f_s.at[yt * chunks + i],
            f_r.at[ys * chunks + i],
            (at(yt, z, c), x),
        )

    def o_copy(zt, zs):
        return remote(zsend.at[zt], gkv_ref.at[zs], o_s.at[zt], o_r.at[zs], (at(y, zt, c), x))

    w_load = pltpu.make_async_copy(w_ref, wbuf, loc_sem.at[0])
    kv_own = pltpu.make_async_copy(
        kv_ref.at[z], kvbuf.at[pl.ds(place(y, c, z), pdev)], loc_sem.at[1]
    )
    q_own = pltpu.make_async_copy(q_ref.at[:, lanes(z)], qbuf.at[z], loc_sem.at[2])
    cot_own = pltpu.make_async_copy(cot_ref, cotbuf.at[x], loc_sem.at[3])
    gq_own = pltpu.make_async_copy(qsend.at[z], gq_ref.at[:, lanes(z)], loc_sem.at[4])
    gkv_own = pltpu.make_async_copy(zsend.at[z], gkv_ref.at[z], loc_sem.at[5])

    barrier = pltpu.get_barrier_semaphore()

    def greet(dev):
        pl.semaphore_signal(barrier, inc=1, device_id=dev, device_id_type=MESH)

    each(1, nz, lambda t: greet((at(y, zat(t), c), x)))
    each(1, ny, lambda t: greet((at(yat(t), z, c), x)))
    each(1, nx, lambda t: greet((me, xat(t))))
    greet((at(y, z, oc), x))
    kv_own.start()
    cot_own.start()
    q_own.start()
    w_load.start()

    live = lax.broadcasted_iota(jnp.int32, (rows, 1), 0) < len_ref[0]
    low_lane = lax.broadcasted_iota(jnp.int32, (1, PAIR), 1) < HS
    low_row = lax.broadcasted_iota(jnp.int32, (PAIR, 1), 0) < HS
    blank = jnp.zeros((1, 1), jnp.bfloat16)

    sg_zero = jnp.zeros((plen, width), jnp.bfloat16)

    def clear(j):
        sg[j, slots] = sg_zero

    each(0, nz, clear)

    step = 256
    cot_own.wait()
    w_load.wait()

    def grad_part(xs, first):
        block = cotbuf[xs]

        def one(n):
            at_n = pl.ds(pl.multiple_of(n * step, step), step)
            weight = wbuf[at_n, pl.ds(pl.multiple_of(xs * cols, cols), cols)]
            part = dot(block, weight, NT)
            if first:
                gacc[:, at_n] = part
            else:
                gacc[:, at_n] += part

        each(0, cols // step, one)

    grad_part(x, True)
    pl.semaphore_wait(barrier, nz + ny + nx - 2)
    each(1, nx, lambda t: x_copy(xat(t), x).start())
    each(1, nz, lambda t: kz_copy(zat(t), z).start())

    kv_own.wait()

    def forward(i):
        def arrived(k):
            zs = i * zper + k

            @pl.when(zs != z)
            def _():
                kz_copy(zs, zs).wait_recv()

        each(0, zper, arrived)
        each(1, ny, lambda t: ky_copy(yat(t), y, i).start())
        kc_copy(y, c, i).start()

    each(0, chunks, forward)
    each(1, nz, lambda t: q_copy(zat(t), z).start())

    def other_part(t):
        xs = xat(t)
        x_copy(xs, xs).wait_recv()
        grad_part(xs, False)

    each(1, nx, other_part)
    for h in range(nz):
        gsend[h] = jnp.where(live, gacc[:, h * PAIR : (h + 1) * PAIR], 0.0).astype(jnp.bfloat16)
    gbuf[z] = gsend[z]
    each(1, nz, lambda t: g_copy(zat(t), z).start())

    def pass_on(t):
        ys = yat(t)

        def one(i):
            ky_copy(ys, ys, i).wait_recv()
            kc_copy(ys, c, i).start()

        each(0, chunks, one)

    each(1, ny, pass_on)
    each(0, ny * chunks, lambda k: kc_copy(k // chunks, oc, lax.rem(k, chunks)).wait_recv())

    q_own.wait()
    tile = 256
    tiles = keys // tile

    def both_rows(block):
        return jnp.concatenate(
            [jnp.where(low_lane, block, blank), jnp.where(low_lane, blank, block)], axis=0
        )

    def both_cols(block):
        return jnp.concatenate(
            [jnp.where(low_row, block, blank), jnp.where(low_row, blank, block)], axis=1
        )

    def pick(wide):
        return jnp.where(low_row, wide[:, :rows], wide[:, rows:])

    def attend(t, lane):
        j = zat(t)
        for k in range(slots):
            kvg[j, k * plen : (k + 1) * plen, :] = kvbuf[ids_ref[k, j]]
        query = both_rows(qbuf[j])
        top = jnp.full((1, 2 * rows), -jnp.inf, jnp.float32)
        for r in range(tiles):
            at_r = pl.ds(r * tile, tile)
            part = dot(kvg[j, at_r, :PAIR], query, NT)
            stbuf[lane, at_r, :] = part
            top = jnp.maximum(top, jnp.max(part, axis=0, keepdims=True))
        total = jnp.zeros((1, 2 * rows), jnp.float32)
        for r in range(tiles):
            at_r = pl.ds(r * tile, tile)
            raised = jnp.exp(stbuf[lane, at_r, :] - top)
            total = total + jnp.sum(raised, axis=0, keepdims=True)
            ebuf[j, at_r, :] = raised.astype(jnp.bfloat16)
        inverse = 1.0 / total
        mixed = dot(kvg[j, :, PAIR:], ebuf[j], TN) * inverse
        mixed = pick(mixed)
        ctxt[j] = mixed
        invl[j] = inverse
        csend[j] = mixed.T.astype(jnp.bfloat16)

    def two(wait, work, send):
        def body(u):
            for t in (2 * u, 2 * u + 1):

                @pl.when(t > 0)
                def _():
                    wait(zat(t))

            for r in range(2):
                work(2 * u + r, r)
            for t in (2 * u, 2 * u + 1):

                @pl.when(t > 0)
                def _():
                    send(zat(t))

        each(0, nz // 2, body)

    two(lambda j: q_copy(j, j).wait_recv(), attend, lambda j: c_copy(j, z).start())
    ctxbuf[:, lanes(z)] = csend[z]

    def grads(t, lane):
        j = zat(t)
        query = both_rows(qbuf[j])
        inverse = jnp.where(low_row, invl[j, :, :rows], invl[j, :, rows:])
        scaled = gbuf[j].astype(jnp.float32).T * inverse
        product = scaled * ctxt[j]
        delta = jnp.concatenate(
            [
                jnp.sum(product[:HS], axis=0, keepdims=True),
                jnp.sum(product[HS:], axis=0, keepdims=True),
            ],
            axis=1,
        )
        wide = both_cols(scaled.astype(jnp.bfloat16))
        for r in range(tiles):
            at_r = pl.ds(r * tile, tile)
            raised = ebuf[j, at_r, :]
            grad = dot(kvg[j, at_r, PAIR:], wide, NN)
            grad = (raised.astype(jnp.float32) * (grad - delta)).astype(jnp.bfloat16)
            dsbuf[lane, at_r, :] = grad
            per = tile // plen
            key_grad = dot(grad, query, NN).astype(jnp.bfloat16)
            value_grad = dot(raised, wide, NT).astype(jnp.bfloat16)
            sg[j, r * per : (r + 1) * per, :, :PAIR] = key_grad.reshape(per, plen, PAIR)
            sg[j, r * per : (r + 1) * per, :, PAIR:] = value_grad.reshape(per, plen, PAIR)
        back = pick(dot(kvg[j, :, :PAIR], dsbuf[lane], TN))
        qsend[j] = back.T.astype(jnp.bfloat16)

    two(lambda j: g_copy(j, j).wait_recv(), grads, lambda j: d_copy(j, z).start())
    gq_own.start()

    def project(xt, own):
        def one(n):
            at_n = pl.ds(pl.multiple_of(n * step, step), step)
            weight = wbuf[:, pl.ds(pl.multiple_of(xt * cols + n * step, step), step)]
            part = jnp.where(live, dot(ctxbuf[...], weight, NN), 0.0)
            if own:
                aown[:, at_n] = part
            else:
                asend[xt, :, at_n] = part.astype(jnp.bfloat16)

        each(0, cols // step, one)

    def project_other(t):
        xt = xat(t)
        project(xt, False)
        a_copy(xt, x).start()

    def gather(p):
        total = sg[0, inv_ref[0, p]].astype(jnp.float32)
        for j in range(1, nz):
            total = total + sg[j, inv_ref[j, p]].astype(jnp.float32)
        return total

    per = zper * pdev

    def for_other_core(i):
        def one(yt):
            for k in range(per):
                cxs[i, yt * per + k] = gather(place(yt, oc, i * zper) + k).astype(jnp.bfloat16)

        each(0, ny, one)
        e_copy(i).start()

    def for_other_y(i):
        e_copy(i).wait_recv()

        def one(yt):
            for k in range(per):
                total = gather(place(yt, c, i * zper) + k) + cxr[i, yt * per + k].astype(jnp.float32)
                ysend[yt, i, k] = total.astype(jnp.bfloat16)

        each(0, ny, one)
        each(1, ny, lambda t: f_copy(yat(t), y, i).start())

    each(0, chunks, for_other_core)
    each(1, nz, lambda t: c_copy(zat(t), zat(t)).wait_recv())
    each(1, 2, project_other)
    each(0, chunks, for_other_y)
    each(2, nx, project_other)

    def finish(i):
        each(1, ny, lambda t: f_copy(yat(t), yat(t), i).wait_recv())

        def one(k):
            zt = i * zper + k
            for r in range(pdev):
                total = ysend[y, i, k * pdev + r].astype(jnp.float32)
                for s in range(1, ny):
                    total = total + yrecv[yat(s), i, k * pdev + r].astype(jnp.float32)
                zsend[zt, r] = total.astype(jnp.bfloat16)

            @pl.when(zt != z)
            def _():
                o_copy(zt, z).start()

        each(0, zper, one)

    each(0, chunks, finish)
    gkv_own.start()

    project(x, True)
    each(1, nx, lambda t: a_copy(xat(t), xat(t)).wait_recv())
    out = aown[...]
    for t in range(1, nx):
        out = out + arecv[xat(t)].astype(jnp.float32)
    att_ref[...] = out.astype(jnp.bfloat16)

    gq_own.wait()
    gkv_own.wait()

    def settle_z(t):
        zt = zat(t)
        d_copy(zt, zt).wait_recv()
        o_copy(zt, zt).wait_recv()
        kz_copy(zt, z).wait_send()
        q_copy(zt, z).wait_send()
        g_copy(zt, z).wait_send()
        c_copy(zt, z).wait_send()
        d_copy(zt, z).wait_send()
        o_copy(zt, z).wait_send()

    each(1, nz, settle_z)

    def settle_y(t):
        each(0, chunks, lambda i: ky_copy(yat(t), y, i).wait_send())
        each(0, chunks, lambda i: f_copy(yat(t), y, i).wait_send())

    each(1, ny, settle_y)
    each(0, ny * chunks, lambda k: kc_copy(k // chunks, c, lax.rem(k, chunks)).wait_send())
    each(0, chunks, lambda i: e_copy(i).wait_send())

    def settle_x(t):
        x_copy(xat(t), x).wait_send()
        a_copy(xat(t), x).wait_send()

    each(1, nx, settle_x)


def local(queries, keys_values, out_weight, cotangent, retrieval, lengths):
    pass_count = lax.axis_size("pass")
    nx = lax.axis_size("tensor")
    me = lax.axis_index("pass")
    pdev, plen, _, cols = keys_values.shape
    rows = queries.shape[0]
    width = out_weight.shape[1]
    slots = retrieval.shape[1]
    nz = cols // PAIR
    ny = pass_count // (nz * CORES)
    passages = pass_count * pdev
    keys = slots * plen

    own = lax.dynamic_slice(
        retrieval.T.reshape(slots, ny, nz, CORES),
        (0, me // (nz * CORES), 0, me % CORES),
        (slots, 1, nz, 1),
    ).reshape(slots, nz)
    holder = own // pdev
    hy, hz, hc = holder // (nz * CORES), (holder // CORES) % nz, holder % CORES
    ids = ((hy * CORES + hc) * nz + hz) * pdev + own % pdev
    match = ids[:, :, None] == jnp.arange(passages)[None, None, :]
    inverse = slots + jnp.sum(
        jnp.where(match, jnp.arange(slots)[:, None, None] - slots, 0), axis=0
    )
    pairs = (
        keys_values.reshape(pdev, plen, 2, nz, PAIR)
        .transpose(3, 0, 1, 2, 4)
        .reshape(nz, pdev, plen, 2 * PAIR)
    )

    bf, f32 = jnp.bfloat16, jnp.float32
    chunks = min(CHUNKS, nz)
    dma = pltpu.SemaphoreType.DMA
    vmem = pltpu.VMEM
    attended, grad_queries, grad_pairs = pl.pallas_call(
        functools.partial(kernel, nx, ny, nz),
        out_shape=(
            jax.ShapeDtypeStruct((rows, cols), bf),
            jax.ShapeDtypeStruct((rows, cols), bf),
            jax.ShapeDtypeStruct((nz, pdev, plen, 2 * PAIR), bf),
        ),
        in_specs=[pl.BlockSpec(memory_space=pltpu.SMEM)] * 3
        + [pl.BlockSpec(memory_space=pltpu.HBM)] * 4,
        out_specs=(
            pl.BlockSpec(memory_space=pltpu.VMEM),
            pl.BlockSpec(memory_space=pl.ANY),
            pl.BlockSpec(memory_space=pl.ANY),
        ),
        scratch_shapes=[
            vmem((passages, plen, 2 * PAIR), bf),
            vmem((nz, rows, PAIR), bf),
            vmem((nz, rows, PAIR), bf),
            vmem((nx, rows, cols), bf),
            vmem((cols, width), bf),
            vmem((rows, cols), f32),
            vmem((nz, rows, PAIR), bf),
            vmem((nz, keys, 2 * PAIR), bf),
            vmem((nz, keys, 2 * rows), bf),
            vmem((2, keys, 2 * rows), bf),
            vmem((2, keys, 2 * rows), f32),
            vmem((nz, PAIR, rows), f32),
            vmem((nz, 1, 2 * rows), f32),
            vmem((nz, rows, PAIR), bf),
            vmem((rows, cols), bf),
            vmem((nz, rows, PAIR), bf),
            vmem((nz, slots + 1, plen, 2 * PAIR), bf),
            vmem((nx, rows, cols), bf),
            vmem((nx, rows, cols), bf),
            vmem((rows, cols), f32),
            vmem((chunks, ny * nz * pdev // chunks, plen, 2 * PAIR), bf),
            vmem((chunks, ny * nz * pdev // chunks, plen, 2 * PAIR), bf),
            vmem((ny, chunks, nz * pdev // chunks, plen, 2 * PAIR), bf),
            vmem((ny, chunks, nz * pdev // chunks, plen, 2 * PAIR), bf),
            vmem((nz, pdev, plen, 2 * PAIR), bf),
            dma((6,)),
        ]
        + [dma((nz,))] * 2
        + [dma((ny * chunks,))] * 4
        + [dma((nz,))] * 8
        + [dma((nx,))] * 4
        + [dma((chunks,))] * 2
        + [dma((ny * chunks,))] * 2
        + [dma((nz,))] * 2,
        compiler_params=pltpu.CompilerParams(
            collective_id=0, has_side_effects=True, vmem_limit_bytes=48 * 1024 * 1024
        ),
    )(ids, inverse, lengths, queries, pairs, out_weight, cotangent)
    grad_keys_values = (
        grad_pairs.reshape(nz, pdev, plen, 2, PAIR)
        .transpose(1, 2, 3, 0, 4)
        .reshape(pdev, plen, 2, cols)
    )
    return (attended, grad_queries, grad_keys_values)


def solution(mesh):
    placed = (
        P("pass", "tensor"),
        P("pass", None, None, "tensor"),
        P("tensor", None),
        P("pass", "tensor"),
        P(),
        P("pass"),
    )
    return jax.shard_map(
        local,
        mesh=mesh,
        in_specs=placed,
        out_specs=(P("pass", "tensor"), P("pass", "tensor"), P("pass", None, None, "tensor")),
        check_vma=False,
    )
```

```python
import functools

import jax
import jax.numpy as jnp
from jax import lax
from jax.experimental import pallas as pl
from jax.experimental.pallas import tpu as pltpu
from jax.sharding import PartitionSpec as P

HS = 64
PAIR = 2 * HS
CORES = 2
CHUNKS = 4
AT_ONCE = 4
MESH = pl.DeviceIdType.MESH
NT = (((1,), (1,)), ((), ()))
TN = (((0,), (0,)), ((), ()))
NN = (((1,), (0,)), ((), ()))


def dot(a, b, dims):
    return lax.dot_general(a, b, dims, preferred_element_type=jnp.float32)


def kernel(
    nx,
    ny,
    nz,
    ids_ref,
    inv_ref,
    len_ref,
    q_ref,
    kv_ref,
    w_ref,
    cot_ref,
    att_ref,
    gq_ref,
    gkv_ref,
    kvbuf,
    qbuf,
    gbuf,
    cotbuf,
    wbuf,
    gacc,
    gsend,
    kvg,
    ebuf,
    dsbuf,
    stbuf,
    ctxt,
    invl,
    csend,
    ctxbuf,
    qsend,
    sg,
    asend,
    arecv,
    aown,
    cxs,
    cxr,
    ysend,
    yrecv,
    yrelay,
    zsend,
    loc_sem,
    kz_s,
    kz_r,
    ky_s,
    ky_r,
    kc_s,
    kc_r,
    q_s,
    q_r,
    g_s,
    g_r,
    c_s,
    c_r,
    d_s,
    d_r,
    x_s,
    x_r,
    a_s,
    a_r,
    e_s,
    e_r,
    f_s,
    f_r,
    r_s,
    r_r,
    o_s,
    o_r,
):
    nc = CORES
    rows = q_ref.shape[0]
    cols = q_ref.shape[1]
    pdev, plen, width = kv_ref.shape[1:]
    slots = ids_ref.shape[0]
    keys = slots * plen
    chunks = min(CHUNKS, nz)
    zper = nz // chunks
    wide_step = min(AT_ONCE, nz)
    me = lax.axis_index("pass")
    x = lax.axis_index("tensor")
    c = lax.rem(me, nc)
    z = lax.rem(me // nc, nz)
    y = me // (nc * nz)
    oc = 1 - c

    def at(yy, zz, cc):
        return (yy * nz + zz) * nc + cc

    def turn(t):
        half = (t + 1) // 2
        return jnp.where(lax.rem(t, 2) == 1, half, -half)

    def zat(t):
        return lax.rem(z + turn(t) + nz, nz)

    def yat(t):
        return lax.rem(y + turn(t) + ny, ny)

    def xat(t):
        return lax.rem(x + turn(t) + nx, nx)

    def place(yy, cc, zz):
        return ((yy * nc + cc) * nz + zz) * pdev

    def remote(src, dst, send, recv, dev):
        return pltpu.make_async_remote_copy(
            src_ref=src,
            dst_ref=dst,
            send_sem=send,
            recv_sem=recv,
            device_id=dev,
            device_id_type=MESH,
        )

    def each(lo, hi, body):
        lax.fori_loop(lo, hi, lambda t, carry: (body(t), carry)[1], 0)

    def lanes(i):
        return pl.ds(pl.multiple_of(i * PAIR, PAIR), PAIR)

    def kz_copy(zt, zs):
        return remote(
            kv_ref.at[zt],
            kvbuf.at[pl.ds(place(y, c, zs), pdev)],
            kz_s.at[zt],
            kz_r.at[zs],
            (at(y, zt, c), x),
        )

    def ky_copy(yt, ys, i):
        part = pl.ds(place(ys, c, i * zper), zper * pdev)
        return remote(
            kvbuf.at[part],
            kvbuf.at[part],
            ky_s.at[yt * chunks + i],
            ky_r.at[ys * chunks + i],
            (at(yt, z, c), x),
        )

    def kc_copy(ys, cs, i):
        part = pl.ds(place(ys, cs, i * zper), zper * pdev)
        return remote(
            kvbuf.at[part],
            kvbuf.at[part],
            kc_s.at[ys * chunks + i],
            kc_r.at[ys * chunks + i],
            (at(y, z, oc), x),
        )

    def q_copy(zt, zs):
        return remote(
            q_ref.at[:, lanes(zt)], qbuf.at[zs], q_s.at[zt], q_r.at[zs], (at(y, zt, c), x)
        )

    def g_copy(zt, zs):
        return remote(
            gsend.at[zt], gbuf.at[zs], g_s.at[zt], g_r.at[zs], (at(y, zt, c), x)
        )

    def c_copy(zt, zs):
        return remote(
            csend.at[zt], ctxbuf.at[:, lanes(zs)], c_s.at[zt], c_r.at[zs], (at(y, zt, c), x)
        )

    def d_copy(zt, zs):
        return remote(
            qsend.at[zt], gq_ref.at[:, lanes(zs)], d_s.at[zt], d_r.at[zs], (at(y, zt, c), x)
        )

    def x_copy(xt, xs):
        return remote(cot_ref, cotbuf.at[xs], x_s.at[xt], x_r.at[xs], (me, xt))

    def a_copy(xt, xs):
        return remote(asend.at[xt], arecv.at[xs], a_s.at[xt], a_r.at[xs], (me, xt))

    def e_copy(i):
        return remote(cxs.at[i], cxr.at[i], e_s.at[i], e_r.at[i], (at(y, z, oc), x))

    def ahead(i):
        return 1 - 2 * lax.rem(i, 2)

    def f_copy(yt, ys, i):
        return remote(
            ysend.at[yt, i],
            yrecv.at[ys, i],
            f_s.at[yt * chunks + i],
            f_r.at[ys * chunks + i],
            (at(yt, z, c), x),
        )

    def r_copy(i):
        return remote(
            ysend.at[lax.rem(y + 2, ny), i],
            yrelay.at[i],
            r_s.at[i],
            r_r.at[i],
            (at(lax.rem(y + ahead(i) + ny, ny), z, c), x),
        )

    def o_copy(zt, zs):
        return remote(zsend.at[zt], gkv_ref.at[zs], o_s.at[zt], o_r.at[zs], (at(y, zt, c), x))

    w_load = pltpu.make_async_copy(w_ref, wbuf, loc_sem.at[0])
    kv_own = pltpu.make_async_copy(
        kv_ref.at[z], kvbuf.at[pl.ds(place(y, c, z), pdev)], loc_sem.at[1]
    )
    q_own = pltpu.make_async_copy(q_ref.at[:, lanes(z)], qbuf.at[z], loc_sem.at[2])
    cot_own = pltpu.make_async_copy(cot_ref, cotbuf.at[x], loc_sem.at[3])
    gq_own = pltpu.make_async_copy(qsend.at[z], gq_ref.at[:, lanes(z)], loc_sem.at[4])
    gkv_own = pltpu.make_async_copy(zsend.at[z], gkv_ref.at[z], loc_sem.at[5])

    barrier = pltpu.get_barrier_semaphore()

    def greet(dev):
        pl.semaphore_signal(barrier, inc=1, device_id=dev, device_id_type=MESH)

    each(1, nz, lambda t: greet((at(y, zat(t), c), x)))
    each(1, ny, lambda t: greet((at(yat(t), z, c), x)))
    each(1, nx, lambda t: greet((me, xat(t))))
    greet((at(y, z, oc), x))
    kv_own.start()
    cot_own.start()
    q_own.start()
    w_load.start()

    live = lax.broadcasted_iota(jnp.int32, (rows, 1), 0) < len_ref[0]
    low_lane = lax.broadcasted_iota(jnp.int32, (1, PAIR), 1) < HS
    low_row = lax.broadcasted_iota(jnp.int32, (PAIR, 1), 0) < HS
    blank = jnp.zeros((1, 1), jnp.bfloat16)

    sg_zero = jnp.zeros((plen, width), jnp.bfloat16)

    def clear(j):
        sg[j, slots] = sg_zero

    each(0, nz, clear)

    step = 256
    cot_own.wait()
    w_load.wait()

    def grad_part(xs, first):
        block = cotbuf[xs]

        def one(n):
            at_n = pl.ds(pl.multiple_of(n * step, step), step)
            weight = wbuf[at_n, pl.ds(pl.multiple_of(xs * cols, cols), cols)]
            part = dot(block, weight, NT)
            if first:
                gacc[:, at_n] = part
            else:
                gacc[:, at_n] += part

        each(0, cols // step, one)

    grad_part(x, True)
    pl.semaphore_wait(barrier, nz + ny + nx - 2)
    each(1, nx, lambda t: x_copy(xat(t), x).start())
    each(1, nz, lambda t: kz_copy(zat(t), z).start())

    kv_own.wait()

    def forward(i):
        def arrived(k):
            zs = i * zper + k

            @pl.when(zs != z)
            def _():
                kz_copy(zs, zs).wait_recv()

        each(0, zper, arrived)
        each(1, ny, lambda t: ky_copy(yat(t), y, i).start())
        kc_copy(y, c, i).start()

    forward(0)
    each(1, nz, lambda t: q_copy(zat(t), z).start())
    each(1, chunks, forward)

    def other_part(t):
        xs = xat(t)
        x_copy(xs, xs).wait_recv()
        grad_part(xs, False)

    if nx > 1:
        each(1, nx - 1, other_part)
        xs = xat(nx - 1)
        x_copy(xs, xs).wait_recv()

    def last_part(n):
        at_n = pl.ds(pl.multiple_of(n * step, step), step)
        part = gacc[:, at_n]
        if nx > 1:
            weight = wbuf[at_n, pl.ds(pl.multiple_of(xs * cols, cols), cols)]
            part = part + dot(cotbuf[xs], weight, NT)
        part = jnp.where(live, part, 0.0).astype(jnp.bfloat16)
        for k in range(step // PAIR):
            h = n * (step // PAIR) + k
            gsend[h] = part[:, k * PAIR : (k + 1) * PAIR]

            @pl.when(h != z)
            def _():
                g_copy(h, z).start()

    each(0, cols // step, last_part)
    gbuf[z] = gsend[z]

    def pass_on(t):
        ys = yat(t)

        def one(i):
            ky_copy(ys, ys, i).wait_recv()
            kc_copy(ys, c, i).start()

        each(0, chunks, one)

    each(1, ny, pass_on)
    each(0, ny * chunks, lambda k: kc_copy(k // chunks, oc, lax.rem(k, chunks)).wait_recv())

    q_own.wait()
    tile = 256
    tiles = keys // tile

    def both_rows(block):
        return jnp.concatenate(
            [jnp.where(low_lane, block, blank), jnp.where(low_lane, blank, block)], axis=0
        )

    def both_cols(block):
        return jnp.concatenate(
            [jnp.where(low_row, block, blank), jnp.where(low_row, blank, block)], axis=1
        )

    def pick(wide):
        return jnp.where(low_row, wide[:, :rows], wide[:, rows:])

    def attend(t, lane):
        j = zat(t)
        for k in range(slots):
            kvg[j, k * plen : (k + 1) * plen, :] = kvbuf[ids_ref[k, j]]
        query = both_rows(qbuf[j])
        top = jnp.full((1, 2 * rows), -jnp.inf, jnp.float32)
        for r in range(tiles):
            at_r = pl.ds(r * tile, tile)
            part = dot(kvg[j, at_r, :PAIR], query, NT)
            stbuf[lane, at_r, :] = part
            top = jnp.maximum(top, jnp.max(part, axis=0, keepdims=True))
        total = jnp.zeros((1, 2 * rows), jnp.float32)
        for r in range(tiles):
            at_r = pl.ds(r * tile, tile)
            raised = jnp.exp(stbuf[lane, at_r, :] - top)
            total = total + jnp.sum(raised, axis=0, keepdims=True)
            ebuf[j, at_r, :] = raised.astype(jnp.bfloat16)
        inverse = 1.0 / total
        mixed = dot(kvg[j, :, PAIR:], ebuf[j], TN) * inverse
        mixed = pick(mixed)
        ctxt[j] = mixed
        invl[j] = inverse
        csend[j] = mixed.T.astype(jnp.bfloat16)

    def batches(wait, work, send):
        def body(u):
            for t in [wide_step * u + r for r in range(wide_step)]:

                @pl.when(t > 0)
                def _():
                    wait(zat(t))

            for r in range(wide_step):
                work(wide_step * u + r, r)
            for t in [wide_step * u + r for r in range(wide_step)]:

                @pl.when(t > 0)
                def _():
                    send(zat(t))

        each(0, nz // wide_step, body)

    batches(lambda j: q_copy(j, j).wait_recv(), attend, lambda j: c_copy(j, z).start())
    ctxbuf[:, lanes(z)] = csend[z]

    def grads(t, lane):
        j = zat(t)
        query = both_rows(qbuf[j])
        inverse = jnp.where(low_row, invl[j, :, :rows], invl[j, :, rows:])
        scaled = gbuf[j].astype(jnp.float32).T * inverse
        product = scaled * ctxt[j]
        delta = jnp.concatenate(
            [
                jnp.sum(product[:HS], axis=0, keepdims=True),
                jnp.sum(product[HS:], axis=0, keepdims=True),
            ],
            axis=1,
        )
        wide = both_cols(scaled.astype(jnp.bfloat16))
        for r in range(tiles):
            at_r = pl.ds(r * tile, tile)
            raised = ebuf[j, at_r, :]
            grad = dot(kvg[j, at_r, PAIR:], wide, NN)
            grad = (raised.astype(jnp.float32) * (grad - delta)).astype(jnp.bfloat16)
            dsbuf[lane, at_r, :] = grad
            per = tile // plen
            key_grad = dot(grad, query, NN).astype(jnp.bfloat16)
            value_grad = dot(raised, wide, NT).astype(jnp.bfloat16)
            sg[j, r * per : (r + 1) * per, :, :PAIR] = key_grad.reshape(per, plen, PAIR)
            sg[j, r * per : (r + 1) * per, :, PAIR:] = value_grad.reshape(per, plen, PAIR)
        back = pick(dot(kvg[j, :, :PAIR], dsbuf[lane], TN))
        qsend[j] = back.T.astype(jnp.bfloat16)

    batches(lambda j: g_copy(j, j).wait_recv(), grads, lambda j: d_copy(j, z).start())
    gq_own.start()

    def project(xt, own):
        def one(n):
            at_n = pl.ds(pl.multiple_of(n * step, step), step)
            weight = wbuf[:, pl.ds(pl.multiple_of(xt * cols + n * step, step), step)]
            part = jnp.where(live, dot(ctxbuf[...], weight, NN), 0.0)
            if own:
                aown[:, at_n] = part
            else:
                asend[xt, :, at_n] = part.astype(jnp.bfloat16)

        each(0, cols // step, one)

    def project_other(t):
        xt = xat(t)
        project(xt, False)
        a_copy(xt, x).start()

    def gather(p):
        total = sg[0, inv_ref[0, p]].astype(jnp.float32)
        for j in range(1, nz):
            total = total + sg[j, inv_ref[j, p]].astype(jnp.float32)
        return total

    per = zper * pdev

    def for_other_core(i):
        def one(yt):
            for k in range(per):
                cxs[i, yt * per + k] = gather(place(yt, oc, i * zper) + k).astype(jnp.bfloat16)

        each(0, ny, one)
        e_copy(i).start()

    def for_other_y(i):
        e_copy(i).wait_recv()

        def one(yt):
            for k in range(per):
                total = gather(place(yt, c, i * zper) + k) + cxr[i, yt * per + k].astype(jnp.float32)
                ysend[yt, i, k] = total.astype(jnp.bfloat16)

        each(0, ny, one)
        r_copy(i).start()
        f_copy(lax.rem(y - ahead(i) + ny, ny), y, i).start()

    def relay(i):
        r_copy(i).wait_recv()
        yt = lax.rem(y + ahead(i) + ny, ny)
        for k in range(per):
            total = ysend[yt, i, k].astype(jnp.float32) + yrelay[i, k].astype(jnp.float32)
            ysend[yt, i, k] = total.astype(jnp.bfloat16)
        f_copy(yt, y, i).start()

    def core_then_y(i):
        for_other_core(i)
        for_other_y(i - 1)

    for_other_core(0)
    each(1, chunks, core_then_y)
    for_other_y(chunks - 1)
    each(1, nz, lambda t: c_copy(zat(t), zat(t)).wait_recv())
    each(1, min(2, nx), project_other)
    each(0, chunks // 2, relay)
    each(2, min(3, nx), project_other)
    each(chunks // 2, chunks, relay)
    each(3, nx, project_other)

    def finish(i):
        each(1, 3, lambda t: f_copy(yat(t), yat(t), i).wait_recv())

        def one(k):
            zt = i * zper + k
            for r in range(pdev):
                total = ysend[y, i, k * pdev + r].astype(jnp.float32)
                for s in range(1, 3):
                    total = total + yrecv[yat(s), i, k * pdev + r].astype(jnp.float32)
                zsend[zt, r] = total.astype(jnp.bfloat16)

            @pl.when(zt != z)
            def _():
                o_copy(zt, z).start()

        each(0, zper, one)

    each(0, chunks, finish)
    gkv_own.start()

    project(x, True)
    each(1, nx, lambda t: a_copy(xat(t), xat(t)).wait_recv())
    out = aown[...]
    for t in range(1, nx):
        out = out + arecv[xat(t)].astype(jnp.float32)
    att_ref[...] = out.astype(jnp.bfloat16)

    gq_own.wait()
    gkv_own.wait()

    def settle_z(t):
        zt = zat(t)
        d_copy(zt, zt).wait_recv()
        o_copy(zt, zt).wait_recv()
        kz_copy(zt, z).wait_send()
        q_copy(zt, z).wait_send()
        g_copy(zt, z).wait_send()
        c_copy(zt, z).wait_send()
        d_copy(zt, z).wait_send()
        o_copy(zt, z).wait_send()

    each(1, nz, settle_z)

    def settle_y(t):
        each(0, chunks, lambda i: ky_copy(yat(t), y, i).wait_send())

    each(1, ny, settle_y)
    each(0, ny * chunks, lambda k: kc_copy(k // chunks, c, lax.rem(k, chunks)).wait_send())
    each(0, chunks, lambda i: e_copy(i).wait_send())
    each(0, chunks, lambda i: r_copy(i).wait_send())
    each(1, 3, lambda t: each(0, chunks, lambda i: f_copy(yat(t), y, i).wait_send()))

    def settle_x(t):
        x_copy(xat(t), x).wait_send()
        a_copy(xat(t), x).wait_send()

    each(1, nx, settle_x)


def local(queries, keys_values, out_weight, cotangent, retrieval, lengths):
    pass_count = lax.axis_size("pass")
    nx = lax.axis_size("tensor")
    me = lax.axis_index("pass")
    pdev, plen, _, cols = keys_values.shape
    rows = queries.shape[0]
    width = out_weight.shape[1]
    slots = retrieval.shape[1]
    nz = cols // PAIR
    ny = pass_count // (nz * CORES)
    passages = pass_count * pdev
    keys = slots * plen

    own = lax.dynamic_slice(
        retrieval.T.reshape(slots, ny, nz, CORES),
        (0, me // (nz * CORES), 0, me % CORES),
        (slots, 1, nz, 1),
    ).reshape(slots, nz)
    holder = own // pdev
    hy, hz, hc = holder // (nz * CORES), (holder // CORES) % nz, holder % CORES
    ids = ((hy * CORES + hc) * nz + hz) * pdev + own % pdev
    match = ids[:, :, None] == jnp.arange(passages)[None, None, :]
    inverse = slots + jnp.sum(
        jnp.where(match, jnp.arange(slots)[:, None, None] - slots, 0), axis=0
    )
    pairs = (
        keys_values.reshape(pdev, plen, 2, nz, PAIR)
        .transpose(3, 0, 1, 2, 4)
        .reshape(nz, pdev, plen, 2 * PAIR)
    )

    bf, f32 = jnp.bfloat16, jnp.float32
    chunks = min(CHUNKS, nz)
    dma = pltpu.SemaphoreType.DMA
    vmem = pltpu.VMEM
    attended, grad_queries, grad_pairs = pl.pallas_call(
        functools.partial(kernel, nx, ny, nz),
        out_shape=(
            jax.ShapeDtypeStruct((rows, cols), bf),
            jax.ShapeDtypeStruct((rows, cols), bf),
            jax.ShapeDtypeStruct((nz, pdev, plen, 2 * PAIR), bf),
        ),
        in_specs=[pl.BlockSpec(memory_space=pltpu.SMEM)] * 3
        + [pl.BlockSpec(memory_space=pltpu.HBM)] * 4,
        out_specs=(
            pl.BlockSpec(memory_space=pltpu.VMEM),
            pl.BlockSpec(memory_space=pl.ANY),
            pl.BlockSpec(memory_space=pl.ANY),
        ),
        scratch_shapes=[
            vmem((passages, plen, 2 * PAIR), bf),
            vmem((nz, rows, PAIR), bf),
            vmem((nz, rows, PAIR), bf),
            vmem((nx, rows, cols), bf),
            vmem((cols, width), bf),
            vmem((rows, cols), f32),
            vmem((nz, rows, PAIR), bf),
            vmem((nz, keys, 2 * PAIR), bf),
            vmem((nz, keys, 2 * rows), bf),
            vmem((min(AT_ONCE, nz), keys, 2 * rows), bf),
            vmem((min(AT_ONCE, nz), keys, 2 * rows), f32),
            vmem((nz, PAIR, rows), f32),
            vmem((nz, 1, 2 * rows), f32),
            vmem((nz, rows, PAIR), bf),
            vmem((rows, cols), bf),
            vmem((nz, rows, PAIR), bf),
            vmem((nz, slots + 1, plen, 2 * PAIR), bf),
            vmem((nx, rows, cols), bf),
            vmem((nx, rows, cols), bf),
            vmem((rows, cols), f32),
            vmem((chunks, ny * nz * pdev // chunks, plen, 2 * PAIR), bf),
            vmem((chunks, ny * nz * pdev // chunks, plen, 2 * PAIR), bf),
            vmem((ny, chunks, nz * pdev // chunks, plen, 2 * PAIR), bf),
            vmem((ny, chunks, nz * pdev // chunks, plen, 2 * PAIR), bf),
            vmem((chunks, nz * pdev // chunks, plen, 2 * PAIR), bf),
            vmem((nz, pdev, plen, 2 * PAIR), bf),
            dma((6,)),
        ]
        + [dma((nz,))] * 2
        + [dma((ny * chunks,))] * 4
        + [dma((nz,))] * 8
        + [dma((nx,))] * 4
        + [dma((chunks,))] * 2
        + [dma((ny * chunks,))] * 2
        + [dma((chunks,))] * 2
        + [dma((nz,))] * 2,
        compiler_params=pltpu.CompilerParams(
            collective_id=0, has_side_effects=True, vmem_limit_bytes=48 * 1024 * 1024
        ),
    )(ids, inverse, lengths, queries, pairs, out_weight, cotangent)
    grad_keys_values = (
        grad_pairs.reshape(nz, pdev, plen, 2, PAIR)
        .transpose(1, 2, 3, 0, 4)
        .reshape(pdev, plen, 2, cols)
    )
    return (attended, grad_queries, grad_keys_values)


def solution(mesh):
    placed = (
        P("pass", "tensor"),
        P("pass", None, None, "tensor"),
        P("tensor", None),
        P("pass", "tensor"),
        P(),
        P("pass"),
    )
    return jax.shard_map(
        local,
        mesh=mesh,
        in_specs=placed,
        out_specs=(P("pass", "tensor"), P("pass", "tensor"), P("pass", None, None, "tensor")),
        check_vma=False,
    )
```

```python
import functools

import jax
import jax.numpy as jnp
from jax import lax
from jax.experimental import pallas as pl
from jax.experimental.pallas import tpu as pltpu
from jax.sharding import PartitionSpec as P

HS = 64
PAIR = 2 * HS
CORES = 2
CHUNKS = 2
AT_ONCE = 4
MESH = pl.DeviceIdType.MESH
NT = (((1,), (1,)), ((), ()))
TN = (((0,), (0,)), ((), ()))
NN = (((1,), (0,)), ((), ()))


def dot(a, b, dims):
    return lax.dot_general(a, b, dims, preferred_element_type=jnp.float32)


def kernel(
    nx,
    ny,
    nz,
    ids_ref,
    inv_ref,
    len_ref,
    q_ref,
    kv_ref,
    w_ref,
    cot_ref,
    att_ref,
    gq_ref,
    gkv_ref,
    kvbuf,
    qbuf,
    gbuf,
    cotbuf,
    wbuf,
    gacc,
    gsend,
    kvg,
    ebuf,
    dsbuf,
    stbuf,
    ctxt,
    invl,
    csend,
    ctxbuf,
    qsend,
    sg,
    asend,
    arecv,
    aown,
    cxs,
    cxr,
    ysend,
    yrecv,
    yrelay,
    zsend,
    loc_sem,
    kz_s,
    kz_r,
    ky_s,
    ky_r,
    kc_s,
    kc_r,
    q_s,
    q_r,
    g_s,
    g_r,
    c_s,
    c_r,
    d_s,
    d_r,
    x_s,
    x_r,
    a_s,
    a_r,
    e_s,
    e_r,
    f_s,
    f_r,
    r_s,
    r_r,
    o_s,
    o_r,
):
    nc = CORES
    rows = q_ref.shape[0]
    cols = q_ref.shape[1]
    pdev, plen, width = kv_ref.shape[1:]
    slots = ids_ref.shape[0]
    keys = slots * plen
    chunks = min(CHUNKS, nz)
    zper = nz // chunks
    wide_step = min(AT_ONCE, nz)
    me = lax.axis_index("pass")
    x = lax.axis_index("tensor")
    c = lax.rem(me, nc)
    z = lax.rem(me // nc, nz)
    y = me // (nc * nz)
    oc = 1 - c

    def at(yy, zz, cc):
        return (yy * nz + zz) * nc + cc

    def turn(t):
        half = (t + 1) // 2
        return jnp.where(lax.rem(t, 2) == 1, half, -half)

    def zat(t):
        return lax.rem(z + turn(t) + nz, nz)

    def yat(t):
        return lax.rem(y + turn(t) + ny, ny)

    def xat(t):
        return lax.rem(x + turn(t) + nx, nx)

    def place(yy, cc, zz):
        return ((yy * nc + cc) * nz + zz) * pdev

    def remote(src, dst, send, recv, dev):
        return pltpu.make_async_remote_copy(
            src_ref=src,
            dst_ref=dst,
            send_sem=send,
            recv_sem=recv,
            device_id=dev,
            device_id_type=MESH,
        )

    def each(lo, hi, body):
        lax.fori_loop(lo, hi, lambda t, carry: (body(t), carry)[1], 0)

    def lanes(i):
        return pl.ds(pl.multiple_of(i * PAIR, PAIR), PAIR)

    def kz_copy(zt, zs):
        return remote(
            kv_ref.at[zt],
            kvbuf.at[pl.ds(place(y, c, zs), pdev)],
            kz_s.at[zt],
            kz_r.at[zs],
            (at(y, zt, c), x),
        )

    def ky_copy(yt, ys, i):
        part = pl.ds(place(ys, c, i * zper), zper * pdev)
        return remote(
            kvbuf.at[part],
            kvbuf.at[part],
            ky_s.at[yt * chunks + i],
            ky_r.at[ys * chunks + i],
            (at(yt, z, c), x),
        )

    def kc_copy(ys, cs, i):
        part = pl.ds(place(ys, cs, i * zper), zper * pdev)
        return remote(
            kvbuf.at[part],
            kvbuf.at[part],
            kc_s.at[ys * chunks + i],
            kc_r.at[ys * chunks + i],
            (at(y, z, oc), x),
        )

    def q_copy(zt, zs):
        return remote(
            q_ref.at[:, lanes(zt)], qbuf.at[zs], q_s.at[zt], q_r.at[zs], (at(y, zt, c), x)
        )

    def g_copy(zt, zs):
        return remote(
            gsend.at[zt], gbuf.at[zs], g_s.at[zt], g_r.at[zs], (at(y, zt, c), x)
        )

    def c_copy(zt, zs):
        return remote(
            csend.at[zt], ctxbuf.at[:, lanes(zs)], c_s.at[zt], c_r.at[zs], (at(y, zt, c), x)
        )

    def d_copy(zt, zs):
        return remote(
            qsend.at[zt], gq_ref.at[:, lanes(zs)], d_s.at[zt], d_r.at[zs], (at(y, zt, c), x)
        )

    def x_copy(xt, xs):
        return remote(cot_ref, cotbuf.at[xs], x_s.at[xt], x_r.at[xs], (me, xt))

    def a_copy(xt, xs):
        return remote(asend.at[xt], arecv.at[xs], a_s.at[xt], a_r.at[xs], (me, xt))

    def e_copy(i):
        return remote(cxs.at[i], cxr.at[i], e_s.at[i], e_r.at[i], (at(y, z, oc), x))

    def ahead(i):
        return 1 - 2 * lax.rem(i, 2)

    def f_copy(yt, ys, i):
        return remote(
            ysend.at[yt, i],
            yrecv.at[ys, i],
            f_s.at[yt * chunks + i],
            f_r.at[ys * chunks + i],
            (at(yt, z, c), x),
        )

    def r_copy(i):
        return remote(
            ysend.at[lax.rem(y + 2, ny), i],
            yrelay.at[i],
            r_s.at[i],
            r_r.at[i],
            (at(lax.rem(y + ahead(i) + ny, ny), z, c), x),
        )

    def o_copy(zt, zs):
        return remote(zsend.at[zt], gkv_ref.at[zs], o_s.at[zt], o_r.at[zs], (at(y, zt, c), x))

    w_load = pltpu.make_async_copy(w_ref, wbuf, loc_sem.at[0])
    kv_own = pltpu.make_async_copy(
        kv_ref.at[z], kvbuf.at[pl.ds(place(y, c, z), pdev)], loc_sem.at[1]
    )
    q_own = pltpu.make_async_copy(q_ref.at[:, lanes(z)], qbuf.at[z], loc_sem.at[2])
    cot_own = pltpu.make_async_copy(cot_ref, cotbuf.at[x], loc_sem.at[3])
    gq_own = pltpu.make_async_copy(qsend.at[z], gq_ref.at[:, lanes(z)], loc_sem.at[4])
    gkv_own = pltpu.make_async_copy(zsend.at[z], gkv_ref.at[z], loc_sem.at[5])

    barrier = pltpu.get_barrier_semaphore()

    def greet(dev):
        pl.semaphore_signal(barrier, inc=1, device_id=dev, device_id_type=MESH)

    each(1, nz, lambda t: greet((at(y, zat(t), c), x)))
    each(1, ny, lambda t: greet((at(yat(t), z, c), x)))
    each(1, nx, lambda t: greet((me, xat(t))))
    greet((at(y, z, oc), x))
    kv_own.start()
    cot_own.start()
    q_own.start()
    w_load.start()

    live = lax.broadcasted_iota(jnp.int32, (rows, 1), 0) < len_ref[0]
    low_lane = lax.broadcasted_iota(jnp.int32, (1, PAIR), 1) < HS
    low_row = lax.broadcasted_iota(jnp.int32, (PAIR, 1), 0) < HS
    blank = jnp.zeros((1, 1), jnp.bfloat16)

    sg_zero = jnp.zeros((plen, width), jnp.bfloat16)

    def clear(j):
        sg[j, slots] = sg_zero

    each(0, nz, clear)

    step = 256
    cot_own.wait()
    w_load.wait()

    def grad_part(xs, first):
        block = cotbuf[xs]

        def one(n):
            at_n = pl.ds(pl.multiple_of(n * step, step), step)
            weight = wbuf[at_n, pl.ds(pl.multiple_of(xs * cols, cols), cols)]
            part = dot(block, weight, NT)
            if first:
                gacc[:, at_n] = part
            else:
                gacc[:, at_n] += part

        each(0, cols // step, one)

    grad_part(x, True)
    pl.semaphore_wait(barrier, nz + ny + nx - 2)
    each(1, nx, lambda t: x_copy(xat(t), x).start())
    each(1, nz, lambda t: kz_copy(zat(t), z).start())

    kv_own.wait()

    def forward(i):
        def arrived(k):
            zs = i * zper + k

            @pl.when(zs != z)
            def _():
                kz_copy(zs, zs).wait_recv()

        each(0, zper, arrived)
        each(1, ny, lambda t: ky_copy(yat(t), y, i).start())
        kc_copy(y, c, i).start()

    forward(0)
    each(1, nz, lambda t: q_copy(zat(t), z).start())
    each(1, chunks, forward)

    def other_part(t):
        xs = xat(t)
        x_copy(xs, xs).wait_recv()
        grad_part(xs, False)

    if nx > 1:
        each(1, nx - 1, other_part)
        xs = xat(nx - 1)
        x_copy(xs, xs).wait_recv()

    def last_part(n):
        at_n = pl.ds(pl.multiple_of(n * step, step), step)
        part = gacc[:, at_n]
        if nx > 1:
            weight = wbuf[at_n, pl.ds(pl.multiple_of(xs * cols, cols), cols)]
            part = part + dot(cotbuf[xs], weight, NT)
        part = jnp.where(live, part, 0.0).astype(jnp.bfloat16)
        for k in range(step // PAIR):
            h = n * (step // PAIR) + k
            gsend[h] = part[:, k * PAIR : (k + 1) * PAIR]

            @pl.when(h != z)
            def _():
                g_copy(h, z).start()

    each(0, cols // step, last_part)
    gbuf[z] = gsend[z]

    def pass_on(t):
        ys = yat(t)

        def one(i):
            ky_copy(ys, ys, i).wait_recv()
            kc_copy(ys, c, i).start()

        each(0, chunks, one)

    each(1, ny, pass_on)
    each(0, ny * chunks, lambda k: kc_copy(k // chunks, oc, lax.rem(k, chunks)).wait_recv())

    q_own.wait()
    tile = 256
    tiles = keys // tile

    def both_rows(block):
        return jnp.concatenate(
            [jnp.where(low_lane, block, blank), jnp.where(low_lane, blank, block)], axis=0
        )

    def both_cols(block):
        return jnp.concatenate(
            [jnp.where(low_row, block, blank), jnp.where(low_row, blank, block)], axis=1
        )

    def pick(wide):
        return jnp.where(low_row, wide[:, :rows], wide[:, rows:])

    def attend(t, lane):
        j = zat(t)
        for k in range(slots):
            kvg[j, k * plen : (k + 1) * plen, :] = kvbuf[ids_ref[k, j]]
        query = both_rows(qbuf[j])
        top = jnp.full((1, 2 * rows), -jnp.inf, jnp.float32)
        for r in range(tiles):
            at_r = pl.ds(r * tile, tile)
            part = dot(kvg[j, at_r, :PAIR], query, NT)
            stbuf[lane, at_r, :] = part
            top = jnp.maximum(top, jnp.max(part, axis=0, keepdims=True))
        total = jnp.zeros((1, 2 * rows), jnp.float32)
        for r in range(tiles):
            at_r = pl.ds(r * tile, tile)
            raised = jnp.exp(stbuf[lane, at_r, :] - top)
            total = total + jnp.sum(raised, axis=0, keepdims=True)
            ebuf[j, at_r, :] = raised.astype(jnp.bfloat16)
        inverse = 1.0 / total
        mixed = dot(kvg[j, :, PAIR:], ebuf[j], TN) * inverse
        mixed = pick(mixed)
        ctxt[j] = mixed
        invl[j] = inverse
        csend[j] = mixed.T.astype(jnp.bfloat16)

    def batches(wait, work, send):
        def body(u):
            for t in [wide_step * u + r for r in range(wide_step)]:

                @pl.when(t > 0)
                def _():
                    wait(zat(t))

            for r in range(wide_step):
                work(wide_step * u + r, r)
            for t in [wide_step * u + r for r in range(wide_step)]:

                @pl.when(t > 0)
                def _():
                    send(zat(t))

        each(0, nz // wide_step, body)

    batches(lambda j: q_copy(j, j).wait_recv(), attend, lambda j: c_copy(j, z).start())
    ctxbuf[:, lanes(z)] = csend[z]

    def grads(t, lane):
        j = zat(t)
        query = both_rows(qbuf[j])
        inverse = jnp.where(low_row, invl[j, :, :rows], invl[j, :, rows:])
        scaled = gbuf[j].astype(jnp.float32).T * inverse
        product = scaled * ctxt[j]
        delta = jnp.concatenate(
            [
                jnp.sum(product[:HS], axis=0, keepdims=True),
                jnp.sum(product[HS:], axis=0, keepdims=True),
            ],
            axis=1,
        )
        wide = both_cols(scaled.astype(jnp.bfloat16))
        for r in range(tiles):
            at_r = pl.ds(r * tile, tile)
            raised = ebuf[j, at_r, :]
            grad = dot(kvg[j, at_r, PAIR:], wide, NN)
            grad = (raised.astype(jnp.float32) * (grad - delta)).astype(jnp.bfloat16)
            dsbuf[lane, at_r, :] = grad
            per = tile // plen
            key_grad = dot(grad, query, NN).astype(jnp.bfloat16)
            value_grad = dot(raised, wide, NT).astype(jnp.bfloat16)
            sg[j, r * per : (r + 1) * per, :, :PAIR] = key_grad.reshape(per, plen, PAIR)
            sg[j, r * per : (r + 1) * per, :, PAIR:] = value_grad.reshape(per, plen, PAIR)
        back = pick(dot(kvg[j, :, :PAIR], dsbuf[lane], TN))
        qsend[j] = back.T.astype(jnp.bfloat16)

    batches(lambda j: g_copy(j, j).wait_recv(), grads, lambda j: d_copy(j, z).start())
    gq_own.start()

    def project(xt, own):
        def one(n):
            at_n = pl.ds(pl.multiple_of(n * step, step), step)
            weight = wbuf[:, pl.ds(pl.multiple_of(xt * cols + n * step, step), step)]
            part = jnp.where(live, dot(ctxbuf[...], weight, NN), 0.0)
            if own:
                aown[:, at_n] = part
            else:
                asend[xt, :, at_n] = part.astype(jnp.bfloat16)

        each(0, cols // step, one)

    def project_other(t):
        xt = xat(t)
        project(xt, False)
        a_copy(xt, x).start()

    def gather(p):
        total = sg[0, inv_ref[0, p]].astype(jnp.float32)
        for j in range(1, nz):
            total = total + sg[j, inv_ref[j, p]].astype(jnp.float32)
        return total

    per = zper * pdev

    def for_other_core(i):
        def one(yt):
            for k in range(per):
                cxs[i, yt * per + k] = gather(place(yt, oc, i * zper) + k).astype(jnp.bfloat16)

        each(0, ny, one)
        e_copy(i).start()

    def for_other_y(i):
        e_copy(i).wait_recv()

        def one(yt):
            for k in range(per):
                total = gather(place(yt, c, i * zper) + k) + cxr[i, yt * per + k].astype(jnp.float32)
                ysend[yt, i, k] = total.astype(jnp.bfloat16)

        each(0, ny, one)
        r_copy(i).start()
        f_copy(lax.rem(y - ahead(i) + ny, ny), y, i).start()

    def relay(i):
        r_copy(i).wait_recv()
        yt = lax.rem(y + ahead(i) + ny, ny)
        for k in range(per):
            total = ysend[yt, i, k].astype(jnp.float32) + yrelay[i, k].astype(jnp.float32)
            ysend[yt, i, k] = total.astype(jnp.bfloat16)
        f_copy(yt, y, i).start()

    def core_then_y(i):
        for_other_core(i)
        for_other_y(i - 1)

    for_other_core(0)
    each(1, chunks, core_then_y)
    for_other_y(chunks - 1)
    each(1, nz, lambda t: c_copy(zat(t), zat(t)).wait_recv())
    each(1, min(2, nx), project_other)
    each(0, chunks // 2, relay)
    each(2, min(3, nx), project_other)
    each(chunks // 2, chunks, relay)
    each(3, nx, project_other)

    def finish(i):
        each(1, 3, lambda t: f_copy(yat(t), yat(t), i).wait_recv())

        def one(k):
            zt = i * zper + k
            for r in range(pdev):
                total = ysend[y, i, k * pdev + r].astype(jnp.float32)
                for s in range(1, 3):
                    total = total + yrecv[yat(s), i, k * pdev + r].astype(jnp.float32)
                zsend[zt, r] = total.astype(jnp.bfloat16)

            @pl.when(zt != z)
            def _():
                o_copy(zt, z).start()

        each(0, zper, one)

    each(0, chunks, finish)
    gkv_own.start()

    project(x, True)
    each(1, nx, lambda t: a_copy(xat(t), xat(t)).wait_recv())
    out = aown[...]
    for t in range(1, nx):
        out = out + arecv[xat(t)].astype(jnp.float32)
    att_ref[...] = out.astype(jnp.bfloat16)

    gq_own.wait()
    gkv_own.wait()

    def settle_z(t):
        zt = zat(t)
        d_copy(zt, zt).wait_recv()
        o_copy(zt, zt).wait_recv()
        kz_copy(zt, z).wait_send()
        q_copy(zt, z).wait_send()
        g_copy(zt, z).wait_send()
        c_copy(zt, z).wait_send()
        d_copy(zt, z).wait_send()
        o_copy(zt, z).wait_send()

    each(1, nz, settle_z)

    def settle_y(t):
        each(0, chunks, lambda i: ky_copy(yat(t), y, i).wait_send())

    each(1, ny, settle_y)
    each(0, ny * chunks, lambda k: kc_copy(k // chunks, c, lax.rem(k, chunks)).wait_send())
    each(0, chunks, lambda i: e_copy(i).wait_send())
    each(0, chunks, lambda i: r_copy(i).wait_send())
    each(1, 3, lambda t: each(0, chunks, lambda i: f_copy(yat(t), y, i).wait_send()))

    def settle_x(t):
        x_copy(xat(t), x).wait_send()
        a_copy(xat(t), x).wait_send()

    each(1, nx, settle_x)


def local(queries, keys_values, out_weight, cotangent, retrieval, lengths):
    pass_count = lax.axis_size("pass")
    nx = lax.axis_size("tensor")
    me = lax.axis_index("pass")
    pdev, plen, _, cols = keys_values.shape
    rows = queries.shape[0]
    width = out_weight.shape[1]
    slots = retrieval.shape[1]
    nz = cols // PAIR
    ny = pass_count // (nz * CORES)
    passages = pass_count * pdev
    keys = slots * plen

    own = lax.dynamic_slice(
        retrieval.T.reshape(slots, ny, nz, CORES),
        (0, me // (nz * CORES), 0, me % CORES),
        (slots, 1, nz, 1),
    ).reshape(slots, nz)
    holder = own // pdev
    hy, hz, hc = holder // (nz * CORES), (holder // CORES) % nz, holder % CORES
    ids = ((hy * CORES + hc) * nz + hz) * pdev + own % pdev
    match = ids[:, :, None] == jnp.arange(passages)[None, None, :]
    inverse = slots + jnp.sum(
        jnp.where(match, jnp.arange(slots)[:, None, None] - slots, 0), axis=0
    )
    pairs = (
        keys_values.reshape(pdev, plen, 2, nz, PAIR)
        .transpose(3, 0, 1, 2, 4)
        .reshape(nz, pdev, plen, 2 * PAIR)
    )

    bf, f32 = jnp.bfloat16, jnp.float32
    chunks = min(CHUNKS, nz)
    dma = pltpu.SemaphoreType.DMA
    vmem = pltpu.VMEM
    attended, grad_queries, grad_pairs = pl.pallas_call(
        functools.partial(kernel, nx, ny, nz),
        out_shape=(
            jax.ShapeDtypeStruct((rows, cols), bf),
            jax.ShapeDtypeStruct((rows, cols), bf),
            jax.ShapeDtypeStruct((nz, pdev, plen, 2 * PAIR), bf),
        ),
        in_specs=[pl.BlockSpec(memory_space=pltpu.SMEM)] * 3
        + [pl.BlockSpec(memory_space=pltpu.HBM)] * 4,
        out_specs=(
            pl.BlockSpec(memory_space=pltpu.VMEM),
            pl.BlockSpec(memory_space=pl.ANY),
            pl.BlockSpec(memory_space=pl.ANY),
        ),
        scratch_shapes=[
            vmem((passages, plen, 2 * PAIR), bf),
            vmem((nz, rows, PAIR), bf),
            vmem((nz, rows, PAIR), bf),
            vmem((nx, rows, cols), bf),
            vmem((cols, width), bf),
            vmem((rows, cols), f32),
            vmem((nz, rows, PAIR), bf),
            vmem((nz, keys, 2 * PAIR), bf),
            vmem((nz, keys, 2 * rows), bf),
            vmem((min(AT_ONCE, nz), keys, 2 * rows), bf),
            vmem((min(AT_ONCE, nz), keys, 2 * rows), f32),
            vmem((nz, PAIR, rows), f32),
            vmem((nz, 1, 2 * rows), f32),
            vmem((nz, rows, PAIR), bf),
            vmem((rows, cols), bf),
            vmem((nz, rows, PAIR), bf),
            vmem((nz, slots + 1, plen, 2 * PAIR), bf),
            vmem((nx, rows, cols), bf),
            vmem((nx, rows, cols), bf),
            vmem((rows, cols), f32),
            vmem((chunks, ny * nz * pdev // chunks, plen, 2 * PAIR), bf),
            vmem((chunks, ny * nz * pdev // chunks, plen, 2 * PAIR), bf),
            vmem((ny, chunks, nz * pdev // chunks, plen, 2 * PAIR), bf),
            vmem((ny, chunks, nz * pdev // chunks, plen, 2 * PAIR), bf),
            vmem((chunks, nz * pdev // chunks, plen, 2 * PAIR), bf),
            vmem((nz, pdev, plen, 2 * PAIR), bf),
            dma((6,)),
        ]
        + [dma((nz,))] * 2
        + [dma((ny * chunks,))] * 4
        + [dma((nz,))] * 8
        + [dma((nx,))] * 4
        + [dma((chunks,))] * 2
        + [dma((ny * chunks,))] * 2
        + [dma((chunks,))] * 2
        + [dma((nz,))] * 2,
        compiler_params=pltpu.CompilerParams(
            collective_id=0, has_side_effects=True, vmem_limit_bytes=48 * 1024 * 1024
        ),
    )(ids, inverse, lengths, queries, pairs, out_weight, cotangent)
    grad_keys_values = (
        grad_pairs.reshape(nz, pdev, plen, 2, PAIR)
        .transpose(1, 2, 3, 0, 4)
        .reshape(pdev, plen, 2, cols)
    )
    return (attended, grad_queries, grad_keys_values)


def solution(mesh):
    placed = (
        P("pass", "tensor"),
        P("pass", None, None, "tensor"),
        P("tensor", None),
        P("pass", "tensor"),
        P(),
        P("pass"),
    )
    return jax.shard_map(
        local,
        mesh=mesh,
        in_specs=placed,
        out_specs=(P("pass", "tensor"), P("pass", "tensor"), P("pass", None, None, "tensor")),
        check_vma=False,
    )
```

```python
import functools

import jax
import jax.numpy as jnp
from jax import lax
from jax.experimental import pallas as pl
from jax.experimental.pallas import tpu as pltpu
from jax.sharding import PartitionSpec as P

HS = 64
PAIR = 2 * HS
CORES = 2
CHUNKS = 2
PARTS = 1
AT_ONCE = 4
MESH = pl.DeviceIdType.MESH
NT = (((1,), (1,)), ((), ()))
TN = (((0,), (0,)), ((), ()))
NN = (((1,), (0,)), ((), ()))


def dot(a, b, dims):
    return lax.dot_general(a, b, dims, preferred_element_type=jnp.float32)


def kernel(
    nx,
    ny,
    nz,
    ids_ref,
    inv_ref,
    len_ref,
    q_ref,
    kv_ref,
    w_ref,
    cot_ref,
    att_ref,
    gq_ref,
    gkv_ref,
    kvbuf,
    qbuf,
    gbuf,
    cotbuf,
    wbuf,
    gacc,
    gsend,
    kvg,
    ebuf,
    dsbuf,
    stbuf,
    ctxt,
    invl,
    csend,
    ctxbuf,
    qsend,
    sg,
    asend,
    arecv,
    aown,
    cxs,
    cxr,
    ysend,
    yrecv,
    yrelay,
    zsend,
    loc_sem,
    kz_s,
    kz_r,
    ky_s,
    ky_r,
    kc_s,
    kc_r,
    q_s,
    q_r,
    g_s,
    g_r,
    c_s,
    c_r,
    d_s,
    d_r,
    x_s,
    x_r,
    a_s,
    a_r,
    e_s,
    e_r,
    f_s,
    f_r,
    r_s,
    r_r,
    o_s,
    o_r,
):
    nc = CORES
    rows = q_ref.shape[0]
    cols = q_ref.shape[1]
    pdev, plen, width = kv_ref.shape[1:]
    slots = ids_ref.shape[0]
    keys = slots * plen
    chunks = min(CHUNKS, nz)
    zper = nz // chunks
    parts = min(PARTS, nz)
    fper = nz // parts
    wide_step = min(AT_ONCE, nz)
    me = lax.axis_index("pass")
    x = lax.axis_index("tensor")
    c = lax.rem(me, nc)
    z = lax.rem(me // nc, nz)
    y = me // (nc * nz)
    oc = 1 - c

    def at(yy, zz, cc):
        return (yy * nz + zz) * nc + cc

    def turn(t):
        half = (t + 1) // 2
        return jnp.where(lax.rem(t, 2) == 1, half, -half)

    def zat(t):
        return lax.rem(z + turn(t) + nz, nz)

    def yat(t):
        return lax.rem(y + turn(t) + ny, ny)

    def xat(t):
        return lax.rem(x + turn(t) + nx, nx)

    def place(yy, cc, zz):
        return ((yy * nc + cc) * nz + zz) * pdev

    def remote(src, dst, send, recv, dev):
        return pltpu.make_async_remote_copy(
            src_ref=src,
            dst_ref=dst,
            send_sem=send,
            recv_sem=recv,
            device_id=dev,
            device_id_type=MESH,
        )

    def each(lo, hi, body):
        lax.fori_loop(lo, hi, lambda t, carry: (body(t), carry)[1], 0)

    def lanes(i):
        return pl.ds(pl.multiple_of(i * PAIR, PAIR), PAIR)

    def kz_copy(zt, zs):
        return remote(
            kv_ref.at[zt],
            kvbuf.at[pl.ds(place(y, c, zs), pdev)],
            kz_s.at[zt],
            kz_r.at[zs],
            (at(y, zt, c), x),
        )

    def ky_copy(yt, ys, i):
        part = pl.ds(place(ys, c, i * fper), fper * pdev)
        return remote(
            kvbuf.at[part],
            kvbuf.at[part],
            ky_s.at[yt * parts + i],
            ky_r.at[ys * parts + i],
            (at(yt, z, c), x),
        )

    def kc_copy(ys, cs, i):
        part = pl.ds(place(ys, cs, i * fper), fper * pdev)
        return remote(
            kvbuf.at[part],
            kvbuf.at[part],
            kc_s.at[ys * parts + i],
            kc_r.at[ys * parts + i],
            (at(y, z, oc), x),
        )

    def q_copy(zt, zs):
        return remote(
            q_ref.at[:, lanes(zt)], qbuf.at[zs], q_s.at[zt], q_r.at[zs], (at(y, zt, c), x)
        )

    def g_copy(zt, zs):
        return remote(
            gsend.at[zt], gbuf.at[zs], g_s.at[zt], g_r.at[zs], (at(y, zt, c), x)
        )

    def c_copy(zt, zs):
        return remote(
            csend.at[zt], ctxbuf.at[:, lanes(zs)], c_s.at[zt], c_r.at[zs], (at(y, zt, c), x)
        )

    def d_copy(zt, zs):
        return remote(
            qsend.at[zt], gq_ref.at[:, lanes(zs)], d_s.at[zt], d_r.at[zs], (at(y, zt, c), x)
        )

    def x_copy(xt, xs):
        return remote(cot_ref, cotbuf.at[xs], x_s.at[xt], x_r.at[xs], (me, xt))

    def a_copy(xt, xs):
        return remote(asend.at[xt], arecv.at[xs], a_s.at[xt], a_r.at[xs], (me, xt))

    def e_copy(i):
        return remote(cxs.at[i], cxr.at[i], e_s.at[i], e_r.at[i], (at(y, z, oc), x))

    def ahead(i):
        return 1 - 2 * lax.rem(i, 2)

    def f_copy(yt, ys, i):
        return remote(
            ysend.at[yt, i],
            yrecv.at[ys, i],
            f_s.at[yt * chunks + i],
            f_r.at[ys * chunks + i],
            (at(yt, z, c), x),
        )

    def r_copy(i):
        return remote(
            ysend.at[lax.rem(y + 2, ny), i],
            yrelay.at[i],
            r_s.at[i],
            r_r.at[i],
            (at(lax.rem(y + ahead(i) + ny, ny), z, c), x),
        )

    def o_copy(zt, zs):
        return remote(zsend.at[zt], gkv_ref.at[zs], o_s.at[zt], o_r.at[zs], (at(y, zt, c), x))

    w_load = pltpu.make_async_copy(w_ref, wbuf, loc_sem.at[0])
    kv_own = pltpu.make_async_copy(
        kv_ref.at[z], kvbuf.at[pl.ds(place(y, c, z), pdev)], loc_sem.at[1]
    )
    q_own = pltpu.make_async_copy(q_ref.at[:, lanes(z)], qbuf.at[z], loc_sem.at[2])
    cot_own = pltpu.make_async_copy(cot_ref, cotbuf.at[x], loc_sem.at[3])
    gq_own = pltpu.make_async_copy(qsend.at[z], gq_ref.at[:, lanes(z)], loc_sem.at[4])
    gkv_own = pltpu.make_async_copy(zsend.at[z], gkv_ref.at[z], loc_sem.at[5])

    barrier = pltpu.get_barrier_semaphore()

    def greet(dev):
        pl.semaphore_signal(barrier, inc=1, device_id=dev, device_id_type=MESH)

    each(1, nz, lambda t: greet((at(y, zat(t), c), x)))
    each(1, ny, lambda t: greet((at(yat(t), z, c), x)))
    each(1, nx, lambda t: greet((me, xat(t))))
    greet((at(y, z, oc), x))
    kv_own.start()
    cot_own.start()
    q_own.start()
    w_load.start()

    live = lax.broadcasted_iota(jnp.int32, (rows, 1), 0) < len_ref[0]
    low_lane = lax.broadcasted_iota(jnp.int32, (1, PAIR), 1) < HS
    low_row = lax.broadcasted_iota(jnp.int32, (PAIR, 1), 0) < HS
    blank = jnp.zeros((1, 1), jnp.bfloat16)

    sg_zero = jnp.zeros((plen, width), jnp.bfloat16)

    def clear(j):
        sg[j, slots] = sg_zero

    each(0, nz, clear)

    step = 256
    cot_own.wait()
    w_load.wait()

    def grad_part(xs, first):
        block = cotbuf[xs]

        def one(n):
            at_n = pl.ds(pl.multiple_of(n * step, step), step)
            weight = wbuf[at_n, pl.ds(pl.multiple_of(xs * cols, cols), cols)]
            part = dot(block, weight, NT)
            if first:
                gacc[:, at_n] = part
            else:
                gacc[:, at_n] += part

        each(0, cols // step, one)

    grad_part(x, True)
    pl.semaphore_wait(barrier, nz + ny + nx - 2)
    each(1, nx, lambda t: x_copy(xat(t), x).start())
    each(1, nz, lambda t: kz_copy(zat(t), z).start())

    kv_own.wait()

    def forward(i):
        def arrived(k):
            zs = i * fper + k

            @pl.when(zs != z)
            def _():
                kz_copy(zs, zs).wait_recv()

        each(0, fper, arrived)
        each(1, ny, lambda t: ky_copy(yat(t), y, i).start())
        kc_copy(y, c, i).start()

    forward(0)
    each(1, nz, lambda t: q_copy(zat(t), z).start())
    each(1, parts, forward)

    def other_part(t):
        xs = xat(t)
        x_copy(xs, xs).wait_recv()
        grad_part(xs, False)

    if nx > 1:
        each(1, nx - 1, other_part)
        xs = xat(nx - 1)
        x_copy(xs, xs).wait_recv()

    def last_part(n):
        at_n = pl.ds(pl.multiple_of(n * step, step), step)
        part = gacc[:, at_n]
        if nx > 1:
            weight = wbuf[at_n, pl.ds(pl.multiple_of(xs * cols, cols), cols)]
            part = part + dot(cotbuf[xs], weight, NT)
        part = jnp.where(live, part, 0.0).astype(jnp.bfloat16)
        for k in range(step // PAIR):
            h = n * (step // PAIR) + k
            gsend[h] = part[:, k * PAIR : (k + 1) * PAIR]

            @pl.when(h != z)
            def _():
                g_copy(h, z).start()

    each(0, cols // step, last_part)
    gbuf[z] = gsend[z]

    def pass_on(t):
        ys = yat(t)

        def one(i):
            ky_copy(ys, ys, i).wait_recv()
            kc_copy(ys, c, i).start()

        each(0, parts, one)

    each(1, ny, pass_on)
    each(0, ny * parts, lambda k: kc_copy(k // parts, oc, lax.rem(k, parts)).wait_recv())

    q_own.wait()
    tile = 256
    tiles = keys // tile

    def both_rows(block):
        return jnp.concatenate(
            [jnp.where(low_lane, block, blank), jnp.where(low_lane, blank, block)], axis=0
        )

    def both_cols(block):
        return jnp.concatenate(
            [jnp.where(low_row, block, blank), jnp.where(low_row, blank, block)], axis=1
        )

    def pick(wide):
        return jnp.where(low_row, wide[:, :rows], wide[:, rows:])

    def attend(t, lane):
        j = zat(t)
        for k in range(slots):
            kvg[j, k * plen : (k + 1) * plen, :] = kvbuf[ids_ref[k, j]]
        query = both_rows(qbuf[j])
        top = jnp.full((1, 2 * rows), -jnp.inf, jnp.float32)
        for r in range(tiles):
            at_r = pl.ds(r * tile, tile)
            part = dot(kvg[j, at_r, :PAIR], query, NT)
            stbuf[lane, at_r, :] = part
            top = jnp.maximum(top, jnp.max(part, axis=0, keepdims=True))
        total = jnp.zeros((1, 2 * rows), jnp.float32)
        for r in range(tiles):
            at_r = pl.ds(r * tile, tile)
            raised = jnp.exp(stbuf[lane, at_r, :] - top)
            total = total + jnp.sum(raised, axis=0, keepdims=True)
            ebuf[j, at_r, :] = raised.astype(jnp.bfloat16)
        inverse = 1.0 / total
        mixed = dot(kvg[j, :, PAIR:], ebuf[j], TN) * inverse
        mixed = pick(mixed)
        ctxt[j] = mixed
        invl[j] = inverse
        csend[j] = mixed.T.astype(jnp.bfloat16)

    def batches(wait, work, send):
        def body(u):
            for t in [wide_step * u + r for r in range(wide_step)]:

                @pl.when(t > 0)
                def _():
                    wait(zat(t))

            for r in range(wide_step):
                work(wide_step * u + r, r)
            for t in [wide_step * u + r for r in range(wide_step)]:

                @pl.when(t > 0)
                def _():
                    send(zat(t))

        each(0, nz // wide_step, body)

    batches(lambda j: q_copy(j, j).wait_recv(), attend, lambda j: c_copy(j, z).start())
    ctxbuf[:, lanes(z)] = csend[z]

    def grads(t, lane):
        j = zat(t)
        query = both_rows(qbuf[j])
        inverse = jnp.where(low_row, invl[j, :, :rows], invl[j, :, rows:])
        scaled = gbuf[j].astype(jnp.float32).T * inverse
        product = scaled * ctxt[j]
        delta = jnp.concatenate(
            [
                jnp.sum(product[:HS], axis=0, keepdims=True),
                jnp.sum(product[HS:], axis=0, keepdims=True),
            ],
            axis=1,
        )
        wide = both_cols(scaled.astype(jnp.bfloat16))
        for r in range(tiles):
            at_r = pl.ds(r * tile, tile)
            raised = ebuf[j, at_r, :]
            grad = dot(kvg[j, at_r, PAIR:], wide, NN)
            grad = (raised.astype(jnp.float32) * (grad - delta)).astype(jnp.bfloat16)
            dsbuf[lane, at_r, :] = grad
            per = tile // plen
            key_grad = dot(grad, query, NN).astype(jnp.bfloat16)
            value_grad = dot(raised, wide, NT).astype(jnp.bfloat16)
            sg[j, r * per : (r + 1) * per, :, :PAIR] = key_grad.reshape(per, plen, PAIR)
            sg[j, r * per : (r + 1) * per, :, PAIR:] = value_grad.reshape(per, plen, PAIR)
        back = pick(dot(kvg[j, :, :PAIR], dsbuf[lane], TN))
        qsend[j] = back.T.astype(jnp.bfloat16)

    batches(lambda j: g_copy(j, j).wait_recv(), grads, lambda j: d_copy(j, z).start())
    gq_own.start()

    def project(xt, own):
        def one(n):
            at_n = pl.ds(pl.multiple_of(n * step, step), step)
            weight = wbuf[:, pl.ds(pl.multiple_of(xt * cols + n * step, step), step)]
            part = jnp.where(live, dot(ctxbuf[...], weight, NN), 0.0)
            if own:
                aown[:, at_n] = part
            else:
                asend[xt, :, at_n] = part.astype(jnp.bfloat16)

        each(0, cols // step, one)

    def project_other(t):
        xt = xat(t)
        project(xt, False)
        a_copy(xt, x).start()

    def gather(p):
        total = sg[0, inv_ref[0, p]].astype(jnp.float32)
        for j in range(1, nz):
            total = total + sg[j, inv_ref[j, p]].astype(jnp.float32)
        return total

    per = zper * pdev

    def for_other_core(i):
        def one(yt):
            for k in range(per):
                cxs[i, yt * per + k] = gather(place(yt, oc, i * zper) + k).astype(jnp.bfloat16)

        each(0, ny, one)
        e_copy(i).start()

    def for_other_y(i):
        e_copy(i).wait_recv()

        def one(yt):
            for k in range(per):
                total = gather(place(yt, c, i * zper) + k) + cxr[i, yt * per + k].astype(jnp.float32)
                ysend[yt, i, k] = total.astype(jnp.bfloat16)

        each(0, ny, one)
        r_copy(i).start()
        f_copy(lax.rem(y - ahead(i) + ny, ny), y, i).start()

    def relay(i):
        r_copy(i).wait_recv()
        yt = lax.rem(y + ahead(i) + ny, ny)
        for k in range(per):
            total = ysend[yt, i, k].astype(jnp.float32) + yrelay[i, k].astype(jnp.float32)
            ysend[yt, i, k] = total.astype(jnp.bfloat16)
        f_copy(yt, y, i).start()

    def core_then_y(i):
        for_other_core(i)
        for_other_y(i - 1)

    for_other_core(0)
    each(1, chunks, core_then_y)
    for_other_y(chunks - 1)
    each(1, nz, lambda t: c_copy(zat(t), zat(t)).wait_recv())
    each(1, min(2, nx), project_other)
    each(0, chunks // 2, relay)
    each(2, min(3, nx), project_other)
    each(chunks // 2, chunks, relay)
    each(3, nx, project_other)

    def finish(i):
        each(1, 3, lambda t: f_copy(yat(t), yat(t), i).wait_recv())

        def one(k):
            zt = i * zper + k
            for r in range(pdev):
                total = ysend[y, i, k * pdev + r].astype(jnp.float32)
                for s in range(1, 3):
                    total = total + yrecv[yat(s), i, k * pdev + r].astype(jnp.float32)
                zsend[zt, r] = total.astype(jnp.bfloat16)

            @pl.when(zt != z)
            def _():
                o_copy(zt, z).start()

        each(0, zper, one)

    each(0, chunks, finish)
    gkv_own.start()

    project(x, True)
    each(1, nx, lambda t: a_copy(xat(t), xat(t)).wait_recv())
    out = aown[...]
    for t in range(1, nx):
        out = out + arecv[xat(t)].astype(jnp.float32)
    att_ref[...] = out.astype(jnp.bfloat16)

    gq_own.wait()
    gkv_own.wait()

    def settle_z(t):
        zt = zat(t)
        d_copy(zt, zt).wait_recv()
        o_copy(zt, zt).wait_recv()
        kz_copy(zt, z).wait_send()
        q_copy(zt, z).wait_send()
        g_copy(zt, z).wait_send()
        c_copy(zt, z).wait_send()
        d_copy(zt, z).wait_send()
        o_copy(zt, z).wait_send()

    each(1, nz, settle_z)

    def settle_y(t):
        each(0, parts, lambda i: ky_copy(yat(t), y, i).wait_send())

    each(1, ny, settle_y)
    each(0, ny * parts, lambda k: kc_copy(k // parts, c, lax.rem(k, parts)).wait_send())
    each(0, chunks, lambda i: e_copy(i).wait_send())
    each(0, chunks, lambda i: r_copy(i).wait_send())
    each(1, 3, lambda t: each(0, chunks, lambda i: f_copy(yat(t), y, i).wait_send()))

    def settle_x(t):
        x_copy(xat(t), x).wait_send()
        a_copy(xat(t), x).wait_send()

    each(1, nx, settle_x)


def local(queries, keys_values, out_weight, cotangent, retrieval, lengths):
    pass_count = lax.axis_size("pass")
    nx = lax.axis_size("tensor")
    me = lax.axis_index("pass")
    pdev, plen, _, cols = keys_values.shape
    rows = queries.shape[0]
    width = out_weight.shape[1]
    slots = retrieval.shape[1]
    nz = cols // PAIR
    ny = pass_count // (nz * CORES)
    passages = pass_count * pdev
    keys = slots * plen

    own = lax.dynamic_slice(
        retrieval.T.reshape(slots, ny, nz, CORES),
        (0, me // (nz * CORES), 0, me % CORES),
        (slots, 1, nz, 1),
    ).reshape(slots, nz)
    holder = own // pdev
    hy, hz, hc = holder // (nz * CORES), (holder // CORES) % nz, holder % CORES
    ids = ((hy * CORES + hc) * nz + hz) * pdev + own % pdev
    match = ids[:, :, None] == jnp.arange(passages)[None, None, :]
    inverse = slots + jnp.sum(
        jnp.where(match, jnp.arange(slots)[:, None, None] - slots, 0), axis=0
    )
    pairs = (
        keys_values.reshape(pdev, plen, 2, nz, PAIR)
        .transpose(3, 0, 1, 2, 4)
        .reshape(nz, pdev, plen, 2 * PAIR)
    )

    bf, f32 = jnp.bfloat16, jnp.float32
    chunks = min(CHUNKS, nz)
    dma = pltpu.SemaphoreType.DMA
    vmem = pltpu.VMEM
    attended, grad_queries, grad_pairs = pl.pallas_call(
        functools.partial(kernel, nx, ny, nz),
        out_shape=(
            jax.ShapeDtypeStruct((rows, cols), bf),
            jax.ShapeDtypeStruct((rows, cols), bf),
            jax.ShapeDtypeStruct((nz, pdev, plen, 2 * PAIR), bf),
        ),
        in_specs=[pl.BlockSpec(memory_space=pltpu.SMEM)] * 3
        + [pl.BlockSpec(memory_space=pltpu.HBM)] * 4,
        out_specs=(
            pl.BlockSpec(memory_space=pltpu.VMEM),
            pl.BlockSpec(memory_space=pl.ANY),
            pl.BlockSpec(memory_space=pl.ANY),
        ),
        scratch_shapes=[
            vmem((passages, plen, 2 * PAIR), bf),
            vmem((nz, rows, PAIR), bf),
            vmem((nz, rows, PAIR), bf),
            vmem((nx, rows, cols), bf),
            vmem((cols, width), bf),
            vmem((rows, cols), f32),
            vmem((nz, rows, PAIR), bf),
            vmem((nz, keys, 2 * PAIR), bf),
            vmem((nz, keys, 2 * rows), bf),
            vmem((min(AT_ONCE, nz), keys, 2 * rows), bf),
            vmem((min(AT_ONCE, nz), keys, 2 * rows), f32),
            vmem((nz, PAIR, rows), f32),
            vmem((nz, 1, 2 * rows), f32),
            vmem((nz, rows, PAIR), bf),
            vmem((rows, cols), bf),
            vmem((nz, rows, PAIR), bf),
            vmem((nz, slots + 1, plen, 2 * PAIR), bf),
            vmem((nx, rows, cols), bf),
            vmem((nx, rows, cols), bf),
            vmem((rows, cols), f32),
            vmem((chunks, ny * nz * pdev // chunks, plen, 2 * PAIR), bf),
            vmem((chunks, ny * nz * pdev // chunks, plen, 2 * PAIR), bf),
            vmem((ny, chunks, nz * pdev // chunks, plen, 2 * PAIR), bf),
            vmem((ny, chunks, nz * pdev // chunks, plen, 2 * PAIR), bf),
            vmem((chunks, nz * pdev // chunks, plen, 2 * PAIR), bf),
            vmem((nz, pdev, plen, 2 * PAIR), bf),
            dma((6,)),
        ]
        + [dma((nz,))] * 2
        + [dma((ny * chunks,))] * 4
        + [dma((nz,))] * 8
        + [dma((nx,))] * 4
        + [dma((chunks,))] * 2
        + [dma((ny * chunks,))] * 2
        + [dma((chunks,))] * 2
        + [dma((nz,))] * 2,
        compiler_params=pltpu.CompilerParams(
            collective_id=0, has_side_effects=True, vmem_limit_bytes=48 * 1024 * 1024
        ),
    )(ids, inverse, lengths, queries, pairs, out_weight, cotangent)
    grad_keys_values = (
        grad_pairs.reshape(nz, pdev, plen, 2, PAIR)
        .transpose(1, 2, 3, 0, 4)
        .reshape(pdev, plen, 2, cols)
    )
    return (attended, grad_queries, grad_keys_values)


def solution(mesh):
    placed = (
        P("pass", "tensor"),
        P("pass", None, None, "tensor"),
        P("tensor", None),
        P("pass", "tensor"),
        P(),
        P("pass"),
    )
    return jax.shard_map(
        local,
        mesh=mesh,
        in_specs=placed,
        out_specs=(P("pass", "tensor"), P("pass", "tensor"), P("pass", None, None, "tensor")),
        check_vma=False,
    )
```
